256 devices in a mesh: view: 64 (over z, y, core), head: 4 (over x).
Axes of the slice: x: 4, y: 4, z: 8, core: 2. Of those that a mesh axis runs over, the one named last changes fastest.
Arguments:
- inputs: bfloat16 [64, 128, 1280], P('view', None, 'head'), may hold values from -6 to 6
- output_gradient: bfloat16 [64, 128, 1280], P('view', None, 'head'), may hold values from -6 to 6
- query_key_value_weight: bfloat16 [3, 1280, 1280], P(None, None, 'head'), may hold values from -0.15625 to 0.15625
- output_weight: bfloat16 [1280, 1280], P('head'), may hold values from -0.15625 to 0.15625
- adapter_down_maps: bfloat16 [3, 1280, 64], replicated, may hold values from -0.15625 to 0.15625
- adapter_up_maps: bfloat16 [3, 64, 1280], P(None, None, 'head'), may hold values from -0.75 to 0.75
- adjacent: int32 [64, 64], P('view'), may hold values from 0 to 1, as said below
Outputs:
- layer_out: bfloat16 [64, 128, 1280], P('view', None, 'head')
- grad_inputs: bfloat16 [64, 128, 1280], P('view', None, 'head')
- grad_a: float32 [3, 1280, 64], P(None, 'head')
- grad_b: float32 [3, 64, 1280], P(None, None, 'head')
The draws below stay inside these ranges and needn't reach their ends.
Inputs may be any that keep to these rules, and one draw needn't show every extreme that they name: adjacent[i, i] is 1; adjacent[i, j] can be 1 only when the circular distance between i and j is at most 8; each row holds at most 16 ones off the diagonal and at least 4 of them; some row holds the most and some row the least.
All inputs are finite; a program needn't handle non-finite values.
Results may differ from the reference program's by a relative error of at most 0.024.
Values may be sent and summed in bfloat16 or wider, within the bound.
A program may use at most 64 MiB of HBM per device.

```python
import jax
import jax.numpy as jnp
from jax import lax

MODEL_WIDTH_SIZE = 1280
H = 20
ADAPTER_RANK = 64
SEQ = 128
VIEWS = 64
RADIUS = 8


def draw_adjacent(key, part):
    key = jax.random.fold_in(key, 7)
    first_key, second_key, third_key, fourth_key = jax.random.split(key, 4)
    view_count = VIEWS
    window = 2 * RADIUS
    lowest = min(4, window - 1)
    degree = jax.random.randint(first_key, (view_count,), lowest, window + 1)
    busiest = jax.random.randint(second_key, (), 0, view_count)
    quietest = (busiest + 1 + jax.random.randint(third_key, (), 0, view_count - 1)) % view_count
    positions = jnp.arange(view_count, dtype=jnp.int32)
    degree = jnp.where(positions == busiest, window, degree)
    degree = jnp.where(positions == quietest, lowest, degree)
    priorities = jax.random.randint(fourth_key, (view_count, window), 0, 1 << 20) * window + jnp.arange(window, dtype=jnp.int32)[None, :]
    ranking = jnp.argsort(jnp.argsort(priorities, axis=1), axis=1)
    chosen = (ranking < degree[:, None]).astype(jnp.int32)
    offsets = jnp.concatenate([jnp.arange(-RADIUS, 0, dtype=jnp.int32), jnp.arange(1, RADIUS + 1, dtype=jnp.int32)])
    targets = (positions[:, None] + offsets[None, :]) % view_count
    hits = (targets[:, :, None] == positions[None, None, :]).astype(jnp.int32) * chosen[:, :, None]
    adjacency = jnp.sum(hits, axis=1) + (positions[:, None] == positions[None, :]).astype(jnp.int32)
    return adjacency.astype(jnp.int32)


def shard_levels(rng, shape, cuts, smallest, largest):
    gain, own = 1.0, jax.random.fold_in(rng, 6)
    for axis_at, parts in cuts:
        draws = jnp.exp(jax.random.uniform(jax.random.fold_in(own, axis_at), (parts,), jnp.float32, smallest / len(cuts), largest / len(cuts)))
        gain = gain * jnp.repeat(draws, shape[axis_at] // parts).reshape([-1 if axis == axis_at else 1 for axis in range(len(shape))])
    return gain


def centred(rng, dims, width, most, cuts=(), held_as=jnp.bfloat16):
    array = jax.random.normal(rng, dims, jnp.float32) * width
    if len(cuts) > 0:
        array = shard_levels(rng, dims, cuts, -0.22, 0.18) * array
    return jnp.clip(array, min=-most, max=most).astype(held_as)


def setup_inputs(seed: int = 0) -> dict:
    arg_keys = jax.random.split(jax.random.key(seed), 8)
    inputs = centred(arg_keys[0], (VIEWS, SEQ, MODEL_WIDTH_SIZE), 1.0, 6.0, ((0, 64), (2, 4)))
    output_gradient = centred(arg_keys[1], (VIEWS, SEQ, MODEL_WIDTH_SIZE), 1.0, 6.0, ((0, 64), (2, 4)))
    query_key_value_weight = centred(arg_keys[2], (3, MODEL_WIDTH_SIZE, MODEL_WIDTH_SIZE), MODEL_WIDTH_SIZE ** -0.5, 0.15625, ((2, 4),))
    output_weight = centred(arg_keys[3], (MODEL_WIDTH_SIZE, MODEL_WIDTH_SIZE), MODEL_WIDTH_SIZE ** -0.5, 0.15625, ((0, 4),))
    adapter_down_maps = centred(arg_keys[4], (3, MODEL_WIDTH_SIZE, ADAPTER_RANK), MODEL_WIDTH_SIZE ** -0.5, 0.15625)
    adapter_up_maps = centred(arg_keys[5], (3, ADAPTER_RANK, MODEL_WIDTH_SIZE), ADAPTER_RANK ** -0.5, 0.75, ((2, 4),))
    adjacent = draw_adjacent(jax.random.fold_in(arg_keys[7], 71), 0)
    return {"inputs": inputs, "output_gradient": output_gradient, "query_key_value_weight": query_key_value_weight, "output_weight": output_weight, "adapter_down_maps": adapter_down_maps, "adapter_up_maps": adapter_up_maps, "adjacent": adjacent}


adapter_scale_factor = 0.5


def rounded(values):
    return lax.optimization_barrier(values.astype(jnp.bfloat16)).astype(jnp.float32)


def reference(inputs, output_gradient, query_key_value_weight, output_weight, adapter_down_maps, adapter_up_maps, adjacent):
    view_count, token_count, model_width = inputs.shape
    head_dim = model_width // H
    flattened_rows = inputs.reshape(view_count * token_count, model_width)
    reduced_features = jnp.stack([jnp.dot(flattened_rows, adapter_down_maps[projection_choice], preferred_element_type=jnp.float32) for projection_choice in range(3)]).astype(jnp.bfloat16)
    projected_rows = jnp.stack([jnp.dot(flattened_rows, query_key_value_weight[projection_choice], preferred_element_type=jnp.float32) + adapter_scale_factor * jnp.dot(reduced_features[projection_choice], adapter_up_maps[projection_choice], preferred_element_type=jnp.float32) for projection_choice in range(3)]).astype(jnp.bfloat16)
    queries = projected_rows[0].reshape(view_count, token_count, H, head_dim)
    keys_all = projected_rows[1].reshape(view_count, token_count, H, head_dim)
    values_all = projected_rows[2].reshape(view_count, token_count, H, head_dim)
    offsets = jnp.arange(-RADIUS, RADIUS + 1, dtype=jnp.int32)
    adjacency = adjacent.astype(jnp.float32)
    inv_scale = head_dim ** -0.5

    def window(view_index):
        indices = ((view_index + offsets) % view_count).astype(jnp.int32)
        return indices, keys_all[indices], values_all[indices], adjacency[view_index, indices]

    def exponents(view_index, key_window, weight):
        logits = jnp.einsum('shd,wthd->hswt', queries[view_index].astype(jnp.float32), key_window.astype(jnp.float32)) * inv_scale
        return jnp.exp(logits) * weight[None, None, :, None]

    def forward_view(view_index):
        indices, key_window, value_window, weight = window(view_index)
        exponent = exponents(view_index, key_window, weight)
        totals = jnp.sum(exponent, axis=(2, 3))
        mixture = jnp.einsum('hswt,wthd->shd', rounded(exponent), value_window.astype(jnp.float32))
        return (mixture / totals.T[:, :, None]).astype(jnp.bfloat16), totals

    attended, totals_all = lax.map(forward_view, jnp.arange(view_count, dtype=jnp.int32))
    layer_out = jnp.dot(attended.reshape(-1, model_width), output_weight, preferred_element_type=jnp.float32).astype(jnp.bfloat16)
    grad_att = jnp.dot(output_gradient.reshape(-1, model_width), output_weight.T, preferred_element_type=jnp.float32).astype(jnp.bfloat16)
    grad_att = grad_att.reshape(view_count, token_count, H, head_dim)

    def backward_view(running, view_index):
        key_acc, value_acc = running
        indices, key_window, value_window, weight = window(view_index)
        exponent = exponents(view_index, key_window, weight)
        probabilities = exponent / totals_all[view_index][:, :, None, None]
        cotangent = grad_att[view_index].astype(jnp.float32)
        dprob = jnp.einsum('shd,wthd->hswt', cotangent, value_window.astype(jnp.float32))
        row_delta = jnp.sum(cotangent * attended[view_index].astype(jnp.float32), axis=2)
        dlogit = rounded(probabilities * (dprob - row_delta.T[:, :, None, None]) * inv_scale)
        query_grad = jnp.einsum('hswt,wthd->shd', dlogit, key_window.astype(jnp.float32))
        key_terms = rounded(jnp.einsum('hswt,shd->wthd', dlogit, queries[view_index].astype(jnp.float32)))
        value_terms = rounded(jnp.einsum('hswt,shd->wthd', rounded(probabilities), cotangent))
        return (key_acc.at[indices].add(key_terms), value_acc.at[indices].add(value_terms)), query_grad

    empty = jnp.zeros((view_count, token_count, H, head_dim), jnp.float32)
    (key_acc, value_acc), query_grads = lax.scan(backward_view, (empty, empty), jnp.arange(view_count, dtype=jnp.int32))
    gradient_list = jnp.stack([query_grads.reshape(-1, model_width), key_acc.reshape(-1, model_width), value_acc.reshape(-1, model_width)]).astype(jnp.bfloat16)
    reduced_gradient = jnp.stack([adapter_scale_factor * jnp.dot(gradient_list[projection_choice], adapter_up_maps[projection_choice].T, preferred_element_type=jnp.float32) for projection_choice in range(3)]).astype(jnp.bfloat16)
    input_sum_total = jnp.zeros((view_count * token_count, model_width), jnp.float32)
    for projection_choice in range(3):
        input_sum_total = input_sum_total + jnp.dot(gradient_list[projection_choice], query_key_value_weight[projection_choice].T, preferred_element_type=jnp.float32)
        input_sum_total = input_sum_total + jnp.dot(reduced_gradient[projection_choice], adapter_down_maps[projection_choice].T, preferred_element_type=jnp.float32)
    grad_inputs = input_sum_total.astype(jnp.bfloat16).reshape(view_count, token_count, model_width)
    grad_a = jnp.stack([jnp.dot(flattened_rows.T, reduced_gradient[projection_choice], preferred_element_type=jnp.float32) for projection_choice in range(3)])
    grad_b = jnp.stack([adapter_scale_factor * jnp.dot(reduced_features[projection_choice].T, gradient_list[projection_choice], preferred_element_type=jnp.float32) for projection_choice in range(3)])
    return layer_out.reshape(view_count, token_count, model_width), grad_inputs, grad_a, grad_b
```

```python
import jax
import jax.numpy as jnp
from jax import lax
from jax.experimental import pallas as pl
from jax.experimental.pallas import tpu as pltpu
from jax.sharding import PartitionSpec as P

MESH = pl.DeviceIdType.MESH
F32 = jnp.float32
BF16 = jnp.bfloat16
T = 128
W = 320
D = 64
R = 64
CHIPS = 32
ROWS = 48


def mm(a, b):
    return lax.dot_general(a, b, (((1,), (0,)), ((), ())), preferred_element_type=F32)


def mm_nt(a, b):
    return lax.dot_general(a, b, (((1,), (1,)), ((), ())), preferred_element_type=F32)


def kernel(
    x_ref, og_ref, adj_ref, wqkv_hbm, wo_hbm, down_hbm, up_hbm,
    lo_ref, gi_ref, ga_ref, gb_ref,
    wqkv, wo, down, up, wsem,
    xs, ogs, xfull, ogfull, xsend, xrecv, ogsend, ogrecv,
    kv, qg, kvsend, kvrecv, kvbsend, kvbrecv, qgsend, qgrecv, qgbsend, qgbrecv,
    st, stown, stsend, strecv,
    aq, ag, a4q, a4g, ak, av, a4kv, wtab,
    est, est4, oacc, o4acc, invb, delb, inv4, del4, dq, dq4, dk, dv, dkv4,
    att, gs, low, inacc, losrc, lobuf, losend, lorecv,
    lgsrc, lgbuf, lgsend, lgrecv, gisrc, gibuf, gisend, girecv,
    acc, accb, rsbuf, rssend, rsrecv, zbuf, zsend, zrecv, fin, finsend, finrecv,
):
    view = lax.axis_index("view")
    head = lax.axis_index("head")
    chip = view // 2
    core = lax.rem(view, 2)
    z = view // 8
    spot = lax.rem(view, 8)
    sgn = 2 * core - 1

    def at(c, k):
        return (lax.rem(c + 2 * CHIPS, CHIPS) * 2 + k, head)

    def step(p, side):
        near = ((p + 1) // 2) * (2 * lax.rem(p, 2) - 1)
        if isinstance(p, int):
            return {7: 4 * side, 8: -4 * side}.get(p, near)
        return jnp.where(p == 7, 4 * side, jnp.where(p == 8, -4 * side, near))

    sibling = (chip * 2 + 1 - core, head)

    def z_peer(o):
        return (lax.rem(z + o, 8) * 8 + spot, head)

    def spot_peer(o):
        return (z * 8 + lax.rem(spot + o, 8), head)

    def x_peer(o):
        return (view, lax.rem(head + o, 4))

    def remote(src, dst, ss, rs, dev):
        return pltpu.make_async_remote_copy(
            src_ref=src, dst_ref=dst, send_sem=ss, recv_sem=rs,
            device_id=dev, device_id_type=MESH,
        )

    weights = [
        pltpu.make_async_copy(s, d, wsem.at[i])
        for i, (s, d) in enumerate(
            ((wqkv_hbm, wqkv), (down_hbm, down), (up_hbm, up), (wo_hbm, wo))
        )
    ]
    for w in weights:
        w.start()

    barrier = pltpu.get_barrier_semaphore()

    def greet(dev):
        pl.semaphore_signal(barrier, inc=1, device_id=dev, device_id_type=MESH)

    for o in (1, 2, 3):
        greet(x_peer(o))

    @pl.loop(1, 9)
    def _(o):
        greet((lax.rem(view + o, 64), head))
        greet((lax.rem(view + 64 - o, 64), head))

    for o in (2, 3, 4, 5, 6):
        greet(z_peer(o))
    pl.semaphore_wait(barrier, 24)

    def x_copy(o):
        return remote(x_ref.at[0], xs.at[head], xsend.at[o], xrecv.at[o], x_peer(o))

    def og_copy(o):
        return remote(og_ref.at[0], ogs.at[head], ogsend.at[o], ogrecv.at[o], x_peer(o))

    for o in (1, 3, 2):
        x_copy(o).start()
    for o in (1, 3, 2):
        og_copy(o).start()
    xs[head] = x_ref[0]
    ogs[head] = og_ref[0]

    adj = adj_ref[...].astype(F32)
    lane64 = lax.broadcasted_iota(jnp.int32, (1, 64), 1)

    def weight_of(v):
        one = jnp.sum(jnp.where(lane64 == v, adj, 0.0), axis=1, keepdims=True)
        return jnp.broadcast_to(one, (1, T))

    for p in range(9):
        c = lax.rem(chip + step(p, sgn) + 2 * CHIPS, CHIPS) * 2
        wtab[p : p + 1, 0:T] = weight_of(c + core)
        wtab[p : p + 1, T : 2 * T] = weight_of(c + 1 - core)
    lane = lax.broadcasted_iota(jnp.int32, (T, T), 1)
    left = lane < D

    def block_diagonal(dst, i, tile):
        zero = jnp.zeros_like(tile)
        dst[i, 0:T, :] = jnp.where(left, tile, zero)
        dst[i, T : 2 * T, :] = jnp.where(left, zero, tile)

    for w in weights[:3]:
        w.wait()
    for o in (1, 2, 3):
        x_copy(o).wait_recv()
    for h in range(4):
        xfull[:, W * h : W * (h + 1)] = xs[h]
    rows = xfull[...]

    def project(m):
        low_m = mm(rows, down[m]).astype(BF16)
        low[m] = low_m
        return (mm(rows, wqkv[m]) + 0.5 * mm(low_m, up[m])).astype(BF16)

    key = project(1)
    value = project(2)
    kv[0:T, 0:256] = key[:, 0:256]
    kv[0:T, 256:512] = value[:, 0:256]
    kv[0:T, 512:576] = key[:, 256:320]
    kv[0:T, 576:640] = value[:, 256:320]

    def pair_rows(p):
        return pl.ds(pl.multiple_of(p * 256, 256), T)

    def sib_rows(p):
        return pl.ds(pl.multiple_of(p * 256 + T, T), T)

    def block_copy(buf, ss, rs, p):
        return remote(
            buf.at[0:T], buf.at[pair_rows(p)], ss.at[p], rs.at[p],
            at(chip - step(p, sgn), core),
        )

    def sib_copy(buf, ss, rs, p, into):
        return remote(
            buf.at[pair_rows(p)], buf.at[sib_rows(into)], ss.at[into], rs.at[into], sibling
        )

    def kv_copy(p):
        return block_copy(kv, kvsend, kvrecv, p)

    def kvb_copy(p, into):
        return sib_copy(kv, kvbsend, kvbrecv, p, into)

    def qg_copy(p):
        return block_copy(qg, qgsend, qgrecv, p)

    def qgb_copy(p, into):
        return sib_copy(qg, qgbsend, qgbrecv, p, into)

    kvb_copy(0, 0).start()

    @pl.loop(1, 9)
    def _(p):
        kv_copy(p).start()

    query = project(0)
    qg[0:T, 0:256] = query[:, 0:256]
    qg[0:T, 512:576] = query[:, 256:320]

    weights[3].wait()
    for o in (1, 2, 3):
        og_copy(o).wait_recv()
    for h in range(4):
        ogfull[:, W * h : W * (h + 1)] = ogs[h]
    grad_att = mm_nt(ogfull[...], wo[...]).astype(BF16)
    qg[0:T, 256:512] = grad_att[:, 0:256]
    qg[0:T, 576:640] = grad_att[:, 256:320]
    qgb_copy(0, 0).start()

    @pl.loop(1, 9)
    def _(p):
        qg_copy(p).start()

    eighth = jnp.asarray(0.125, BF16)
    for i in range(2):
        block_diagonal(aq, i, qg[0:T, T * i : T * (i + 1)] * eighth)
        block_diagonal(ag, i, qg[0:T, 256 + T * i : 256 + T * (i + 1)])
        block_diagonal(ak, i, kv[0:T, T * i : T * (i + 1)] * eighth)
        block_diagonal(av, i, kv[0:T, 256 + T * i : 256 + T * (i + 1)])
    tile = qg[0:T, 512:640]
    a4q[...] = jnp.where(left, tile * eighth, jnp.zeros_like(tile))
    a4g[...] = jnp.where(left, jnp.zeros_like(tile), tile)
    tile = kv[0:T, 512:640]
    a4kv[0:T, :] = jnp.where(left, tile * eighth, jnp.zeros_like(tile))
    a4kv[T : 2 * T, :] = jnp.where(left, jnp.zeros_like(tile), tile)

    oacc[...] = jnp.zeros_like(oacc)
    o4acc[...] = jnp.zeros_like(o4acc)
    dq[...] = jnp.zeros_like(dq)
    dq4[...] = jnp.zeros_like(dq4)
    dk[...] = jnp.zeros_like(dk)
    dv[...] = jnp.zeros_like(dv)
    dkv4[...] = jnp.zeros_like(dkv4)

    def block(buf, p, n):
        span = pl.ds(pl.multiple_of(p * 256, 256), n)
        return [buf[span, T * i : T * (i + 1)] for i in range(5)]

    def forward(p, n):
        k0, k1, v0, v1, kv4 = block(kv, p, n)
        weight = wtab[pl.ds(p, 1), 0:n]
        ones = jnp.ones((n, T), BF16)
        for i, (k, v) in enumerate(((k0, v0), (k1, v1))):
            e = (jnp.exp(mm_nt(aq[i], k)) * weight).astype(BF16)
            est[p, i, :, 0:n] = e
            oacc[i] += mm(e, jnp.concatenate([v, ones], axis=1))
        e = (jnp.exp(mm_nt(a4q[...], kv4)) * weight).astype(BF16)
        est4[p, :, 0:n] = e
        o4acc[...] += mm(e, jnp.concatenate([kv4, ones], axis=1))

    @pl.loop(1, 7)
    def _(p):
        kv_copy(p).wait_recv()
        kvb_copy(p, p).start()
        kvb_copy(p - 1, p - 1).wait_recv()
        forward(p - 1, 256)

    kv_copy(8).wait_recv()
    kvb_copy(8, 7).start()
    kvb_copy(6, 6).wait_recv()
    forward(6, 256)
    forward(8, T)
    kv_copy(7).wait_recv()
    kvb_copy(8, 7).wait_recv()
    forward(7, 256)

    def diagonal(a):
        return jnp.where(left, a[0:T], a[T : 2 * T])

    stats = jnp.zeros((T, T), F32)

    def put(stats, i, column):
        return jnp.where(lane == i, column, stats)

    for i in range(2):
        inv = 1.0 / oacc[i, :, T : 2 * T]
        invb[i] = inv
        pair = diagonal(oacc[i, :, 0:T] * inv).astype(BF16)
        att[:, T * i : T * (i + 1)] = pair
        prod = pair.astype(F32) * qg[0:T, 256 + T * i : 256 + T * (i + 1)].astype(F32)
        first = jnp.sum(jnp.where(left, prod, 0.0), axis=1, keepdims=True)
        second = jnp.sum(jnp.where(left, 0.0, prod), axis=1, keepdims=True)
        delb[i, 0:T, :] = jnp.broadcast_to(first, (T, T))
        delb[i, T : 2 * T, :] = jnp.broadcast_to(second, (T, T))
        stats = put(stats, 2 * i, inv[0:T])
        stats = put(stats, 2 * i + 1, inv[T : 2 * T])
        stats = put(stats, 5 + 2 * i, first)
        stats = put(stats, 6 + 2 * i, second)
    inv = 1.0 / o4acc[:, T : 2 * T]
    inv4[...] = inv
    last = (o4acc[:, 0:T] * inv).astype(BF16)
    att[:, 256:320] = last[:, D:T]
    prod = last.astype(F32) * qg[0:T, 512:640].astype(F32)
    first = jnp.sum(jnp.where(left, 0.0, prod), axis=1, keepdims=True)
    del4[...] = jnp.broadcast_to(first, (T, T))
    stats = put(stats, 4, inv)
    stats = put(stats, 9, first)
    stown[...] = jnp.transpose(stats)[0:16, :]
    stown[10:11, 0:64] = adj

    def st_copy(p):
        return remote(
            stown, st.at[p, 0], stsend.at[p, 0], strecv.at[p, 0],
            at(chip - step(p, sgn), core),
        )

    def stb_copy(p):
        return remote(
            stown, st.at[p, 1], stsend.at[p, 1], strecv.at[p, 1],
            at(chip - step(p, -sgn), 1 - core),
        )

    @pl.loop(0, 8)
    def _(p):
        st_copy(p + 1).start()
        stb_copy(p).start()

    st[0, 0] = stown[...]

    share = mm(att[...], wo[...]).astype(BF16)
    for h in range(4):
        losrc[h] = share[:, W * h : W * (h + 1)]

    def lo_copy(o):
        return remote(
            losrc.at[lax.rem(head + o, 4)], lobuf.at[o], losend.at[o], lorecv.at[o], x_peer(o)
        )

    for o in (1, 2, 3):
        lo_copy(o).start()

    def wide(a, n):
        return a if n == T else jnp.concatenate([a, a], axis=1)

    def backward_q(p, n):
        k0, k1, v0, v1, kv4 = block(kv, p, n)
        for i, (k, v) in enumerate(((k0, v0), (k1, v1))):
            prob = est[p, i, :, 0:n].astype(F32) * wide(invb[i], n)
            dl = prob * (mm_nt(ag[i], v) - wide(delb[i], n))
            dq[i] += mm(dl.astype(BF16), k)
        prob = est4[p, :, 0:n].astype(F32) * wide(inv4[...], n)
        dl = prob * (mm_nt(a4g[...], kv4) - wide(del4[...], n))
        dq4[...] += mm(dl.astype(BF16), kv4)

    backward_q(0, 256)

    @pl.loop(1, 7)
    def _(p):
        qg_copy(p).wait_recv()
        qgb_copy(p, p).start()
        backward_q(p, 256)

    qg_copy(8).wait_recv()
    qgb_copy(8, 7).start()
    backward_q(7, 256)
    backward_q(8, T)
    for i in range(2):
        gs[0, :, T * i : T * (i + 1)] = (diagonal(dq[i]) * 0.125).astype(BF16)
    gs[0, :, 256:320] = (dq4[:, 0:D] * 0.125).astype(BF16)
    inacc[...] = mm_nt(gs[0], wqkv[0])

    me_lane = lax.broadcasted_iota(jnp.int32, (1, T), 1) == view

    def backward_kv(p, n):
        q0, q1, g0, g1, qg4 = block(qg, p, n)
        sides = [st[p, s] for s in range(n // T)]
        invs, deltas = [], []
        for s in sides:
            w = jnp.sum(jnp.where(me_lane, s[10:11, :], 0.0), axis=1, keepdims=True)
            invs.append(s * w)
        invs = invs[0] if n == T else jnp.concatenate(invs, axis=1)
        deltas = sides[0] if n == T else jnp.concatenate(sides, axis=1)

        def weigh(e, h):
            return e * invs[h : h + 1, :]

        def shift(dp, h):
            return dp - deltas[5 + h : 6 + h, :]

        for i, (q, g) in enumerate(((q0, g0), (q1, g1))):
            e = jnp.exp(mm_nt(ak[i], q))
            dp = mm_nt(av[i], g)
            prob = [weigh(e[0:T], 2 * i), weigh(e[T : 2 * T], 2 * i + 1)]
            dl = [prob[0] * shift(dp[0:T], 2 * i), prob[1] * shift(dp[T : 2 * T], 2 * i + 1)]
            prob = jnp.concatenate(prob, axis=0).astype(BF16)
            dl = jnp.concatenate(dl, axis=0).astype(BF16)
            dk[i] += mm(dl, q)
            dv[i] += mm(prob, g)
        both = mm_nt(a4kv[...], qg4)
        prob = weigh(jnp.exp(both[0:T]), 4)
        dl = prob * shift(both[T : 2 * T], 4)
        dkv4[...] += mm(jnp.concatenate([dl, prob], axis=0).astype(BF16), qg4)

    def st_wait(p):
        st_copy(p).wait_recv()

    stb_copy(0).wait_recv()
    qgb_copy(0, 0).wait_recv()
    backward_kv(0, 256)

    @pl.loop(1, 7)
    def _(p):
        qgb_copy(p, p).wait_recv()
        st_copy(p).wait_recv()
        stb_copy(p).wait_recv()
        backward_kv(p, 256)

    st_copy(8).wait_recv()
    backward_kv(8, T)
    st_copy(7).wait_recv()
    stb_copy(7).wait_recv()
    qg_copy(7).wait_recv()
    qgb_copy(8, 7).wait_recv()
    backward_kv(7, 256)

    for i in range(2):
        gs[1, :, T * i : T * (i + 1)] = (diagonal(dk[i]) * 0.125).astype(BF16)
        gs[2, :, T * i : T * (i + 1)] = diagonal(dv[i]).astype(BF16)
    gs[1, :, 256:320] = (dkv4[0:T, 0:D] * 0.125).astype(BF16)
    gs[2, :, 256:320] = dkv4[T : 2 * T, D:T].astype(BF16)

    for m in range(3):
        lgsrc[R * m : R * (m + 1), :] = (0.5 * mm_nt(up[m], gs[m])).astype(BF16)

    def lg_copy(o):
        return remote(lgsrc, lgbuf.at[o], lgsend.at[o], lgrecv.at[o], x_peer(o))

    for o in (1, 2, 3):
        lg_copy(o).start()

    share = (inacc[...] + mm_nt(gs[1], wqkv[1]) + mm_nt(gs[2], wqkv[2])).astype(BF16)
    for h in range(4):
        gisrc[h] = share[:, W * h : W * (h + 1)]

    def gi_copy(o):
        return remote(
            gisrc.at[lax.rem(head + o, 4)], gibuf.at[o], gisend.at[o], girecv.at[o], x_peer(o)
        )

    for o in (1, 2, 3):
        gi_copy(o).start()
    for m in range(3):
        acc[3 * R + R * m : 3 * R + R * (m + 1), :] = 0.5 * mm(
            jnp.transpose(low[m].astype(F32)).astype(BF16), gs[m]
        )

    for o in (1, 2, 3):
        lg_copy(o).wait_recv()
    lg = lgsrc[...].astype(F32)
    for o in (1, 2, 3):
        lg = lg + lgbuf[o].astype(F32)
    lg = lg.astype(BF16)
    for m in range(3):
        acc[R * m : R * (m + 1), :] = mm(lg[R * m : R * (m + 1), :], x_ref[0])

    accb[...] = acc[...].astype(BF16)

    def share_rows(i):
        return pl.ds(pl.multiple_of(i * ROWS, 16), ROWS)

    def rs_copy(o):
        return remote(
            accb.at[share_rows(lax.rem(spot + o, 8))], rsbuf.at[o],
            rssend.at[o], rsrecv.at[o], spot_peer(o),
        )

    for o in range(1, 8):
        rs_copy(o).start()

    own = jnp.zeros((T, W), F32)
    lgt = jnp.transpose(lg.astype(F32)).astype(BF16)
    for m in range(3):
        part = down[m, pl.ds(pl.multiple_of(head * W, 64), W), :]
        own = own + mm_nt(lgt[:, R * m : R * (m + 1)], part)
    own = own + gisrc[head].astype(F32)
    for o in (1, 2, 3):
        gi_copy(o).wait_recv()
        own = own + gibuf[o].astype(F32)
    gi_ref[0] = own.astype(BF16)
    out = losrc[head].astype(F32)
    for o in (1, 2, 3):
        lo_copy(o).wait_recv()
        out = out + lobuf[o].astype(F32)
    lo_ref[0] = out.astype(BF16)

    total = acc[share_rows(spot), :]
    for o in range(1, 8):
        rs_copy(o).wait_recv()
        total = total + rsbuf[o].astype(F32)
    zbuf[z] = total.astype(BF16)

    def z_copy(o):
        return remote(zbuf.at[z], zbuf.at[z], zsend.at[o], zrecv.at[o], z_peer(o))

    for o in range(1, 8):
        z_copy(o).start()
    for o in range(1, 8):
        z_copy(o).wait_recv()
    total = zbuf[0].astype(F32)
    for i in range(1, 8):
        total = total + zbuf[i].astype(F32)
    fin[spot] = total.astype(BF16)

    def fin_copy(o):
        return remote(fin.at[spot], fin.at[spot], finsend.at[o], finrecv.at[o], spot_peer(o))

    for o in range(1, 8):
        fin_copy(o).start()
    for o in range(1, 8):
        fin_copy(o).wait_recv()
    for i in range(4):
        first = i * ROWS
        for r in range(0, ROWS, 16):
            m, at_row = divmod(first + r, R)
            ga_ref[m, at_row : at_row + 16, :] = fin[i, r : r + 16, :].astype(F32)
            gb_ref[m, at_row : at_row + 16, :] = fin[i + 4, r : r + 16, :].astype(F32)

    for o in (1, 2, 3):
        x_copy(o).wait_send()
        og_copy(o).wait_send()
        lo_copy(o).wait_send()
        lg_copy(o).wait_send()
        gi_copy(o).wait_send()

    @pl.loop(1, 9)
    def _(p):
        kv_copy(p).wait_send()
        qg_copy(p).wait_send()
        st_copy(p).wait_send()
        stb_copy(p - 1).wait_send()

    @pl.loop(0, 7)
    def _(p):
        kvb_copy(p, p).wait_send()
        qgb_copy(p, p).wait_send()

    kvb_copy(8, 7).wait_send()
    qgb_copy(8, 7).wait_send()
    for o in range(1, 8):
        rs_copy(o).wait_send()
        z_copy(o).wait_send()
        fin_copy(o).wait_send()


def body(inputs, output_gradient, wqkv, wo, down, up, adjacent):
    vmem = pltpu.VMEM
    dma = pltpu.SemaphoreType.DMA
    scratch = [
        vmem((3, 1280, W), BF16), vmem((W, 1280), BF16), vmem((3, 1280, R), BF16),
        vmem((3, R, W), BF16), dma((4,)),
        vmem((4, T, W), BF16), vmem((4, T, W), BF16), vmem((T, 1280), BF16),
        vmem((T, 1280), BF16), dma((4,)), dma((4,)), dma((4,)), dma((4,)),
        vmem((17 * T, 640), BF16), vmem((17 * T, 640), BF16),
        dma((9,)), dma((9,)), dma((8,)), dma((8,)), dma((9,)), dma((9,)), dma((8,)), dma((8,)),
        vmem((9, 2, 16, T), F32), vmem((16, T), F32), dma((9, 2)), dma((9, 2)),
        vmem((2, 256, T), BF16), vmem((2, 256, T), BF16), vmem((T, T), BF16), vmem((T, T), BF16),
        vmem((2, 256, T), BF16), vmem((2, 256, T), BF16), vmem((256, T), BF16),
        vmem((16, 256), F32),
        vmem((9, 2, 256, 256), BF16), vmem((9, T, 256), BF16), vmem((2, 256, 256), F32),
        vmem((T, 256), F32), vmem((2, 256, T), F32), vmem((2, 256, T), F32), vmem((T, T), F32),
        vmem((T, T), F32), vmem((2, 256, T), F32), vmem((T, T), F32), vmem((2, 256, T), F32),
        vmem((2, 256, T), F32), vmem((256, T), F32),
        vmem((T, W), BF16), vmem((3, T, W), BF16), vmem((3, T, R), BF16), vmem((T, 1280), F32),
        vmem((4, T, W), BF16), vmem((4, T, W), BF16), dma((4,)), dma((4,)),
        vmem((3 * R, T), BF16), vmem((4, 3 * R, T), BF16), dma((4,)), dma((4,)),
        vmem((4, T, W), BF16), vmem((4, T, W), BF16), dma((4,)), dma((4,)),
        vmem((6 * R, W), F32), vmem((6 * R, W), BF16), vmem((8, ROWS, W), BF16), dma((8,)),
        dma((8,)), vmem((8, ROWS, W), BF16), dma((8,)), dma((8,)), vmem((8, ROWS, W), BF16),
        dma((8,)), dma((8,)),
    ]
    whole = pl.BlockSpec(memory_space=pltpu.VMEM)
    anywhere = pl.BlockSpec(memory_space=pl.ANY)
    layer_out, grad_inputs, grad_a, grad_b = pl.pallas_call(
        kernel,
        out_shape=(
            jax.ShapeDtypeStruct((1, T, W), BF16),
            jax.ShapeDtypeStruct((1, T, W), BF16),
            jax.ShapeDtypeStruct((3, R, W), F32),
            jax.ShapeDtypeStruct((3, R, W), F32),
        ),
        in_specs=[whole] * 3 + [anywhere] * 4,
        out_specs=(whole,) * 4,
        scratch_shapes=scratch,
        compiler_params=pltpu.CompilerParams(
            collective_id=0, has_side_effects=True, vmem_limit_bytes=48 * 1024 * 1024
        ),
        name="layer",
    )(inputs, output_gradient, adjacent, wqkv, wo, down, up)
    return layer_out, grad_inputs, jnp.swapaxes(grad_a, 1, 2), grad_b


def solution(mesh):
    return jax.shard_map(
        body,
        mesh=mesh,
        in_specs=(
            P("view", None, "head"),
            P("view", None, "head"),
            P(None, None, "head"),
            P("head", None),
            P(),
            P(None, None, "head"),
            P("view", None),
        ),
        out_specs=(
            P("view", None, "head"),
            P("view", None, "head"),
            P(None, "head", None),
            P(None, None, "head"),
        ),
        check_vma=False,
    )
```

```python
import jax
import jax.numpy as jnp
from jax import lax
from jax.experimental import pallas as pl
from jax.experimental.pallas import tpu as pltpu
from jax.sharding import PartitionSpec as P

MESH = pl.DeviceIdType.MESH
F32 = jnp.float32
BF16 = jnp.bfloat16
T = 128
W = 320
D = 64
R = 64
ORDER = (0, 1, 2, 8, 5, 6, 7, 3, 4)
CHIPS = 32


def mm(a, b):
    return lax.dot_general(a, b, (((1,), (0,)), ((), ())), preferred_element_type=F32)


def mm_nt(a, b):
    return lax.dot_general(a, b, (((1,), (1,)), ((), ())), preferred_element_type=F32)


def kernel(
    adj_ref, x_hbm, og_hbm, wqkv_hbm, wo_hbm, down_hbm, up_hbm,
    lo_ref, gi_ref, ga_ref, gb_ref,
    wqkv, wo, down, up, wsem,
    xt, ogt, upt, downn, xsend, xrecv, ogsend, ogrecv,
    kv, qg, kvsend, kvrecv, kvbsend, kvbrecv, qgsend, qgrecv, qgbsend, qgbrecv,
    st, stsend, strecv,
    aq, ag, a4q, a4g, ak, av, a4kv, wtab,
    est, est4, oacc, o4acc, invb, delb, inv4, del4, dq, dq4, dk, dv, dkv4,
    att, gs, low, inacc, losrc, lobuf, losend, lorecv,
    gisrc, gibuf, gisend, girecv, lgall, *parts,
):
    view = lax.axis_index("view")
    head = lax.axis_index("head")
    chip = view // 2
    core = lax.rem(view, 2)
    z = view // 8
    y = lax.rem(chip, 4)
    spot = lax.rem(view, 8)
    sgn = 2 * core - 1

    def at(c, k):
        return (lax.rem(c + 2 * CHIPS, CHIPS) * 2 + k, head)

    def step(p, side):
        near = ((p + 1) // 2) * (2 * lax.rem(p, 2) - 1)
        if isinstance(p, int):
            return {7: 4 * side, 8: -4 * side}.get(p, near)
        return jnp.where(p == 7, 4 * side, jnp.where(p == 8, -4 * side, near))

    sibling = (chip * 2 + 1 - core, head)

    def z_peer(o):
        return (lax.rem(z + o, 8) * 8 + spot, head)

    def spot_peer(o):
        return (z * 8 + lax.rem(spot + o, 8), head)

    def x_peer(o):
        return (view, lax.rem(head + o, 4))

    def remote(src, dst, ss, rs, dev):
        return pltpu.make_async_remote_copy(
            src_ref=src, dst_ref=dst, send_sem=ss, recv_sem=rs,
            device_id=dev, device_id_type=MESH,
        )

    mine = pl.ds(pl.multiple_of(head * W, 64), W)
    loads = [
        pltpu.make_async_copy(s, d, wsem.at[i])
        for i, (s, d) in enumerate(
            (
                (x_hbm.at[0], xt.at[mine]), (down_hbm, down), (up_hbm, up), (wqkv_hbm, wqkv),
                (og_hbm.at[0], ogt.at[mine]), (wo_hbm, wo),
            )
        )
    ]
    for load in loads:
        load.start()

    barrier = pltpu.get_barrier_semaphore()

    def greet(dev):
        pl.semaphore_signal(barrier, inc=1, device_id=dev, device_id_type=MESH)

    for o in (1, 2, 3):
        greet(x_peer(o))

    @pl.loop(1, 9)
    def _(o):
        greet((lax.rem(view + o, 64), head))
        greet((lax.rem(view + 64 - o, 64), head))

    for o in (2, 3, 4, 5, 6):
        greet(z_peer(o))
    pl.semaphore_wait(barrier, 24)

    def x_copy(o):
        return remote(x_hbm.at[0], xt.at[mine], xsend.at[o], xrecv.at[o], x_peer(o))

    def og_copy(o):
        return remote(og_hbm.at[0], ogt.at[mine], ogsend.at[o], ogrecv.at[o], x_peer(o))

    for o in (1, 3, 2):
        x_copy(o).start()

    adj = adj_ref[...].astype(F32)
    lane64 = lax.broadcasted_iota(jnp.int32, (1, 64), 1)

    def weight_of(v):
        one = jnp.sum(jnp.where(lane64 == v, adj, 0.0), axis=1, keepdims=True)
        return jnp.broadcast_to(one, (1, T))

    for p in range(9):
        c = lax.rem(chip + step(p, sgn) + 2 * CHIPS, CHIPS) * 2
        wtab[p : p + 1, 0:T] = weight_of(c + core)
        wtab[p : p + 1, T : 2 * T] = weight_of(c + 1 - core)
    lane = lax.broadcasted_iota(jnp.int32, (T, T), 1)
    left = lane < D

    def block_diagonal(dst, i, tile):
        zero = jnp.zeros_like(tile)
        dst[i, 0:T, :] = jnp.where(left, tile, zero)
        dst[i, T : 2 * T, :] = jnp.where(left, zero, tile)

    for load in loads[1:3]:
        load.wait()
    for m in range(3):
        upt[m] = jnp.transpose(up[R * m : R * (m + 1), :])
    for h in range(10):
        downn[T * h : T * (h + 1), :] = jnp.transpose(down[:, T * h : T * (h + 1)])

    loads[3].wait()
    loads[0].wait()
    for o in (1, 2, 3):
        x_copy(o).wait_recv()
    for o in (1, 3, 2):
        og_copy(o).start()
    low[...] = mm(down[...], xt[...]).astype(BF16)

    def project(m):
        main = mm(wqkv[W * m : W * (m + 1), :], xt[...])
        return (main + 0.5 * mm(upt[m], low[R * m : R * (m + 1), :])).astype(BF16)

    def lay_out(buf, first, second):
        for i in range(2):
            part = slice(T * i, T * (i + 1))
            buf[0:T, T * i : T * (i + 1)] = jnp.transpose(first[part])
            buf[0:T, 256 + T * i : 256 + T * (i + 1)] = jnp.transpose(second[part])
        both = jnp.concatenate([first[256:320], second[256:320]], axis=0)
        buf[0:T, 512:640] = jnp.transpose(both)

    lay_out(kv, project(1), project(2))

    def pair_rows(p):
        return pl.ds(pl.multiple_of(p * 256, 256), T)

    def sib_rows(p):
        return pl.ds(pl.multiple_of(p * 256 + T, T), T)

    def sib_copy(buf, ss, rs, p, into):
        return remote(
            buf.at[pair_rows(p)], buf.at[sib_rows(into)], ss.at[into], rs.at[into], sibling
        )

    class Blocks:
        def __init__(self, buf, ss, rs, bs, br):
            self.buf, self.ss, self.rs, self.bs, self.br = buf, ss, rs, bs, br

        def copy(self, p):
            return remote(
                self.buf.at[0:T], self.buf.at[pair_rows(p)], self.ss.at[p], self.rs.at[p],
                at(chip - step(p, sgn), core),
            )

        def start_own(self):
            self.sib(0).start()
            for p in ORDER[1:]:
                self.copy(p).start()

        def sib(self, p):
            return sib_copy(self.buf, self.bs, self.br, p, 7 if p == 8 else p)

        def arrive(self, *ps):
            for p in ps:
                self.copy(p).wait_recv()
                if p != 7:
                    self.sib(p).start()

        def sib_arrived(self, p):
            if p != 8:
                self.sib(8 if p == 7 else p).wait_recv()

        def drain(self):
            for p in range(9):
                if p > 0:
                    self.copy(p).wait_send()
                if p != 7:
                    self.sib(p).wait_send()

    keys = Blocks(kv, kvsend, kvrecv, kvbsend, kvbrecv)
    queries = Blocks(qg, qgsend, qgrecv, qgbsend, qgbrecv)
    keys.start_own()
    query = project(0)
    loads[5].wait()
    loads[4].wait()
    for o in (1, 2, 3):
        og_copy(o).wait_recv()
    lay_out(qg, query, mm(wo[...], ogt[...]).astype(BF16))
    queries.start_own()

    eighth = jnp.asarray(0.125, BF16)
    for i in range(2):
        block_diagonal(aq, i, qg[0:T, T * i : T * (i + 1)] * eighth)
        block_diagonal(ag, i, qg[0:T, 256 + T * i : 256 + T * (i + 1)])
        block_diagonal(ak, i, kv[0:T, T * i : T * (i + 1)] * eighth)
        block_diagonal(av, i, kv[0:T, 256 + T * i : 256 + T * (i + 1)])
    tile = qg[0:T, 512:640]
    a4q[...] = jnp.where(left, tile * eighth, jnp.zeros_like(tile))
    a4g[...] = jnp.where(left, jnp.zeros_like(tile), tile)
    tile = kv[0:T, 512:640]
    a4kv[0:T, :] = jnp.where(left, tile * eighth, jnp.zeros_like(tile))
    a4kv[T : 2 * T, :] = jnp.where(left, jnp.zeros_like(tile), tile)

    oacc[...] = jnp.zeros_like(oacc)
    o4acc[...] = jnp.zeros_like(o4acc)
    dq[...] = jnp.zeros_like(dq)
    dq4[...] = jnp.zeros_like(dq4)
    dk[...] = jnp.zeros_like(dk)
    dv[...] = jnp.zeros_like(dv)
    dkv4[...] = jnp.zeros_like(dkv4)

    def block(buf, p, n):
        span = pl.ds(pl.multiple_of(p * 256, 256), n)
        return [buf[span, T * i : T * (i + 1)] for i in range(5)]

    def forward(p, n):
        k0, k1, v0, v1, kv4 = block(kv, p, n)
        weight = wtab[pl.ds(p, 1), 0:n]
        ones = jnp.ones((n, T), BF16)
        for i, (k, v) in enumerate(((k0, v0), (k1, v1))):
            e = (jnp.exp(mm_nt(aq[i], k)) * weight).astype(BF16)
            est[p, i, :, 0:n] = e
            oacc[i] += mm(e, jnp.concatenate([v, ones], axis=1))
        e = (jnp.exp(mm_nt(a4q[...], kv4)) * weight).astype(BF16)
        est4[p, :, 0:n] = e
        o4acc[...] += mm(e, jnp.concatenate([kv4, ones], axis=1))

    def run(work, blocks, order):
        for p in order:
            if blocks is not None:
                blocks.sib_arrived(p)
            work(p, T if p == 8 else 256)

    previous = 0
    for p in ORDER[1:]:
        keys.arrive(p)
        run(forward, keys, (previous,))
        previous = p
    run(forward, keys, (previous,))

    def diagonal(a):
        return jnp.where(left, a[0:T], a[T : 2 * T])

    stats = jnp.zeros((T, T), F32)

    def put(stats, i, column):
        return jnp.where(lane == i, column, stats)

    for i in range(2):
        inv = 1.0 / oacc[i, :, T : 2 * T]
        invb[i] = inv
        pair = diagonal(oacc[i, :, 0:T] * inv).astype(BF16)
        att[:, T * i : T * (i + 1)] = pair
        prod = pair.astype(F32) * qg[0:T, 256 + T * i : 256 + T * (i + 1)].astype(F32)
        first = jnp.sum(jnp.where(left, prod, 0.0), axis=1, keepdims=True)
        second = jnp.sum(jnp.where(left, 0.0, prod), axis=1, keepdims=True)
        delb[i, 0:T, :] = jnp.broadcast_to(first, (T, T))
        delb[i, T : 2 * T, :] = jnp.broadcast_to(second, (T, T))
        stats = put(stats, 2 * i, inv[0:T])
        stats = put(stats, 2 * i + 1, inv[T : 2 * T])
        stats = put(stats, 5 + 2 * i, first)
        stats = put(stats, 6 + 2 * i, second)
    inv = 1.0 / o4acc[:, T : 2 * T]
    inv4[...] = inv
    last = (o4acc[:, 0:T] * inv).astype(BF16)
    att[:, 256:320] = last[:, D:T]
    prod = last.astype(F32) * qg[0:T, 512:640].astype(F32)
    first = jnp.sum(jnp.where(left, 0.0, prod), axis=1, keepdims=True)
    del4[...] = jnp.broadcast_to(first, (T, T))
    stats = put(stats, 4, inv)
    stats = put(stats, 9, first)
    st[0, 0] = jnp.transpose(stats)[0:16, :]
    st[0, 0, 10:11, 0:64] = adj

    def stb_copy():
        return remote(st.at[0, 0], st.at[0, 1], stsend.at[0], strecv.at[0], sibling)

    def st_copy(p):
        return remote(
            st.at[0], st.at[p], stsend.at[p], strecv.at[p], at(chip - step(p, sgn), core)
        )

    stb_copy().start()
    stb_copy().wait_recv()
    for p in ORDER[1:]:
        st_copy(p).start()

    share = mm(att[...], wo[...]).astype(BF16)
    for h in range(4):
        losrc[h] = share[:, W * h : W * (h + 1)]

    def lo_copy(o):
        return remote(
            losrc.at[lax.rem(head + o, 4)], lobuf.at[o], losend.at[o], lorecv.at[o], x_peer(o)
        )

    for o in (1, 2, 3):
        lo_copy(o).start()

    def wide(a, n):
        return a if n == T else jnp.concatenate([a, a], axis=1)

    def backward_q(p, n):
        k0, k1, v0, v1, kv4 = block(kv, p, n)
        for i, (k, v) in enumerate(((k0, v0), (k1, v1))):
            prob = est[p, i, :, 0:n].astype(F32) * wide(invb[i], n)
            dl = prob * (mm_nt(ag[i], v) - wide(delb[i], n))
            dq[i] += mm(dl.astype(BF16), k)
        prob = est4[p, :, 0:n].astype(F32) * wide(inv4[...], n)
        dl = prob * (mm_nt(a4g[...], kv4) - wide(del4[...], n))
        dq4[...] += mm(dl.astype(BF16), kv4)

    run(backward_q, None, ORDER)
    for i in range(2):
        gs[0, :, T * i : T * (i + 1)] = (diagonal(dq[i]) * 0.125).astype(BF16)
    gs[0, :, 256:320] = (dq4[:, 0:D] * 0.125).astype(BF16)

    class Adapters:
        def __init__(self, which, lgsrc, lgbuf, acc, accb, rsbuf, zbuf, fin, sems):
            self.which, self.lgsrc, self.lgbuf = which, lgsrc, lgbuf
            self.acc, self.accb, self.rsbuf, self.zbuf, self.fin = acc, accb, rsbuf, zbuf, fin
            self.sems = sems
            self.count = R * len(which)
            self.share = self.count // 4

        def part(self, i):
            return pl.ds(pl.multiple_of(i * self.share, 16), self.share)

        def copies(self, stage):
            def copy(o):
                ends = {
                    0: lambda: (self.lgsrc, self.lgbuf.at[o], x_peer(o)),
                    1: lambda: (
                        self.accb.at[self.part(lax.rem(spot + o, 8))], self.rsbuf.at[o], spot_peer(o)
                    ),
                    2: lambda: (self.zbuf.at[z], self.zbuf.at[z], z_peer(o)),
                    3: lambda: (self.fin.at[spot], self.fin.at[spot], spot_peer(o)),
                }
                src, dst, dev = ends[stage]()
                return remote(src, dst, self.sems.at[stage, 0, o], self.sems.at[stage, 1, o], dev)

            return [copy(o) for o in range(1, 8 if stage else 4)]

        def start(self, stage):
            for c in self.copies(stage):
                c.start()

        def wait(self, stage):
            for c in self.copies(stage):
                c.wait_recv()

        def send_low(self):
            for i, m in enumerate(self.which):
                one = 0.5 * mm_nt(up[R * m : R * (m + 1), :], gs[m])
                self.lgsrc[R * i : R * (i + 1), :] = one.astype(BF16)
            self.start(0)
            for i, m in enumerate(self.which):
                self.acc[self.count + R * i : self.count + R * (i + 1), :] = 0.5 * mm(
                    low[R * m : R * (m + 1), :], gs[m]
                )

        def send_plane(self):
            self.wait(0)
            lg = self.lgsrc[...].astype(F32)
            for o in (1, 2, 3):
                lg = lg + self.lgbuf[o].astype(F32)
            lg = lg.astype(BF16)
            lgall[R * self.which[0] : R * self.which[0] + self.count, :] = lg
            self.acc[0 : self.count, :] = mm_nt(lg, xt[mine, :])
            self.accb[...] = self.acc[...].astype(BF16)
            self.start(1)

        def send_z(self):
            self.wait(1)
            total = self.acc[self.part(spot), :]
            for o in range(1, 8):
                total = total + self.rsbuf[o].astype(F32)
            self.zbuf[z] = total.astype(BF16)
            self.start(2)

        def send_back(self):
            self.wait(2)
            total = self.zbuf[0].astype(F32)
            for i in range(1, 8):
                total = total + self.zbuf[i].astype(F32)
            self.fin[spot] = total.astype(BF16)
            self.start(3)

        def finish(self):
            self.wait(3)
            for i in range(8):
                for r in range(0, self.share, 16):
                    which, at_row = divmod((i % 4) * self.share + r, R)
                    out = ga_ref if i < 4 else gb_ref
                    rows = slice(at_row, at_row + 16)
                    out[self.which[which], rows, :] = self.fin[i, r : r + 16, :].astype(F32)

        def drain(self):
            for stage in range(4):
                for c in self.copies(stage):
                    c.wait_send()

    late = Adapters((0, 1, 2), *parts)
    inacc[...] = mm(gs[0], wqkv[0:W, :])

    me_lane = lax.broadcasted_iota(jnp.int32, (1, T), 1) == view

    def backward_kv(p, n):
        q0, q1, g0, g1, qg4 = block(qg, p, n)
        sides = [st[p, s] for s in range(n // T)]
        invs, deltas = [], []
        for s in sides:
            w = jnp.sum(jnp.where(me_lane, s[10:11, :], 0.0), axis=1, keepdims=True)
            invs.append(s * w)
        invs = invs[0] if n == T else jnp.concatenate(invs, axis=1)
        deltas = sides[0] if n == T else jnp.concatenate(sides, axis=1)

        def weigh(e, h):
            return e * invs[h : h + 1, :]

        def shift(dp, h):
            return dp - deltas[5 + h : 6 + h, :]

        for i, (q, g) in enumerate(((q0, g0), (q1, g1))):
            e = jnp.exp(mm_nt(ak[i], q))
            dp = mm_nt(av[i], g)
            prob = [weigh(e[0:T], 2 * i), weigh(e[T : 2 * T], 2 * i + 1)]
            dl = [prob[0] * shift(dp[0:T], 2 * i), prob[1] * shift(dp[T : 2 * T], 2 * i + 1)]
            prob = jnp.concatenate(prob, axis=0).astype(BF16)
            dl = jnp.concatenate(dl, axis=0).astype(BF16)
            dk[i] += mm(dl, q)
            dv[i] += mm(prob, g)
        both = mm_nt(a4kv[...], qg4)
        prob = weigh(jnp.exp(both[0:T]), 4)
        dl = prob * shift(both[T : 2 * T], 4)
        dkv4[...] += mm(jnp.concatenate([dl, prob], axis=0).astype(BF16), qg4)

    def run_kv(*order):
        for p in order:
            if p != 0:
                st_copy(p).wait_recv()
        run(backward_kv, queries, order)

    queries.arrive(1, 2, 8, 5, 6, 7, 3, 4)
    run_kv(*ORDER)
    for i in range(2):
        gs[1, :, T * i : T * (i + 1)] = (diagonal(dk[i]) * 0.125).astype(BF16)
        gs[2, :, T * i : T * (i + 1)] = diagonal(dv[i]).astype(BF16)
    gs[1, :, 256:320] = (dkv4[0:T, 0:D] * 0.125).astype(BF16)
    gs[2, :, 256:320] = dkv4[T : 2 * T, D:T].astype(BF16)

    late.send_low()

    share = inacc[...] + mm(gs[1], wqkv[W : 2 * W, :]) + mm(gs[2], wqkv[2 * W : 3 * W, :])
    share = share.astype(BF16)
    for h in range(4):
        gisrc[h] = share[:, W * h : W * (h + 1)]

    def gi_copy(o):
        return remote(
            gisrc.at[lax.rem(head + o, 4)], gibuf.at[o], gisend.at[o], girecv.at[o], x_peer(o)
        )

    for o in (1, 2, 3):
        gi_copy(o).start()
    late.send_plane()

    own = gisrc[head].astype(F32)
    for o in (1, 2, 3):
        gi_copy(o).wait_recv()
        own = own + gibuf[o].astype(F32)
    gi_ref[0] = (jnp.transpose(own) + mm(downn[mine, :], lgall[...])).astype(BF16)
    out = losrc[head].astype(F32)
    for o in (1, 2, 3):
        lo_copy(o).wait_recv()
        out = out + lobuf[o].astype(F32)
    lo_ref[0] = jnp.transpose(out).astype(BF16)

    late.send_z()
    late.send_back()
    late.finish()

    for o in (1, 2, 3):
        x_copy(o).wait_send()
        og_copy(o).wait_send()
        lo_copy(o).wait_send()
        gi_copy(o).wait_send()
    keys.drain()
    queries.drain()

    stb_copy().wait_send()
    for p in ORDER[1:]:
        st_copy(p).wait_send()
    late.drain()


def hand_over(*refs):
    source, target, held, sem = refs[0:4], refs[4:8], refs[8:12], refs[12]
    into = [pltpu.make_async_copy(s, h, sem.at[0, i]) for i, (s, h) in enumerate(zip(source, held))]
    out = [pltpu.make_async_copy(h, t, sem.at[1, i]) for i, (h, t) in enumerate(zip(held, target))]
    for copy in into:
        copy.start()
    for first, second in zip(into, out):
        first.wait()
        second.start()
    for copy in out:
        copy.wait()


def body(inputs, output_gradient, wqkv, wo, down, up, adjacent):
    vmem = pltpu.VMEM
    dma = pltpu.SemaphoreType.DMA
    scratch = [
        vmem((3 * W, 1280), BF16), vmem((W, 1280), BF16), vmem((3 * R, 1280), BF16),
        vmem((3 * R, W), BF16), dma((6,)),
        vmem((1280, T), BF16), vmem((1280, T), BF16), vmem((3, W, R), BF16),
        vmem((1280, 3 * R), BF16), dma((4,)), dma((4,)), dma((4,)), dma((4,)),
        vmem((17 * T, 640), BF16), vmem((17 * T, 640), BF16),
        dma((9,)), dma((9,)), dma((8,)), dma((8,)), dma((9,)), dma((9,)), dma((8,)), dma((8,)),
        vmem((9, 2, 16, T), F32), dma((9,)), dma((9,)),
        vmem((2, 256, T), BF16), vmem((2, 256, T), BF16), vmem((T, T), BF16), vmem((T, T), BF16),
        vmem((2, 256, T), BF16), vmem((2, 256, T), BF16), vmem((256, T), BF16),
        vmem((16, 256), F32),
        vmem((9, 2, 256, 256), BF16), vmem((9, T, 256), BF16), vmem((2, 256, 256), F32),
        vmem((T, 256), F32), vmem((2, 256, T), F32), vmem((2, 256, T), F32), vmem((T, T), F32),
        vmem((T, T), F32), vmem((2, 256, T), F32), vmem((T, T), F32), vmem((2, 256, T), F32),
        vmem((2, 256, T), F32), vmem((256, T), F32),
        vmem((T, W), BF16), vmem((3, T, W), BF16), vmem((3 * R, T), BF16), vmem((T, 1280), F32),
        vmem((4, T, W), BF16), vmem((4, T, W), BF16), dma((4,)), dma((4,)),
        vmem((4, T, W), BF16), vmem((4, T, W), BF16), dma((4,)), dma((4,)), vmem((3 * R, T), BF16),
    ]
    share = vmem((8, 6 * R // 8, W), BF16)
    scratch += [vmem((3 * R, T), BF16), vmem((4, 3 * R, T), BF16), vmem((6 * R, W), F32)]
    scratch += [vmem((6 * R, W), BF16), share, share, share, dma((4, 2, 8))]
    whole = pl.BlockSpec(memory_space=pltpu.VMEM)
    hbm = pl.BlockSpec(memory_space=pltpu.HBM)
    results = pl.pallas_call(
        kernel,
        out_shape=(
            jax.ShapeDtypeStruct((1, W, T), BF16),
            jax.ShapeDtypeStruct((1, W, T), BF16),
            jax.ShapeDtypeStruct((3, R, W), F32),
            jax.ShapeDtypeStruct((3, R, W), F32),
        ),
        in_specs=[whole] + [hbm] * 6,
        out_specs=(whole,) * 4,
        scratch_shapes=scratch,
        compiler_params=pltpu.CompilerParams(
            collective_id=0, has_side_effects=True, vmem_limit_bytes=62 * 1024 * 1024
        ),
        name="layer",
    )(
        adjacent,
        jnp.swapaxes(inputs, 1, 2),
        jnp.swapaxes(output_gradient, 1, 2),
        jnp.swapaxes(wqkv, 1, 2).reshape(3 * W, 1280),
        wo,
        jnp.swapaxes(down, 1, 2).reshape(3 * R, 1280),
        up.reshape(3 * R, W),
    )
    layer_out, grad_inputs, grad_a, grad_b = pl.pallas_call(
        hand_over,
        out_shape=tuple(jax.ShapeDtypeStruct(r.shape, r.dtype) for r in results),
        in_specs=[hbm] * 4,
        out_specs=(hbm,) * 4,
        scratch_shapes=[vmem(r.shape, r.dtype) for r in results] + [dma((2, 4))],
        compiler_params=pltpu.CompilerParams(vmem_limit_bytes=62 * 1024 * 1024),
        name="hand_over",
    )(*results)
    return (
        jnp.swapaxes(layer_out, 1, 2),
        jnp.swapaxes(grad_inputs, 1, 2),
        jnp.swapaxes(grad_a, 1, 2),
        grad_b,
    )


def solution(mesh):
    return jax.shard_map(
        body,
        mesh=mesh,
        in_specs=(
            P("view", None, "head"),
            P("view", None, "head"),
            P(None, None, "head"),
            P("head", None),
            P(),
            P(None, None, "head"),
            P("view", None),
        ),
        out_specs=(
            P("view", None, "head"),
            P("view", None, "head"),
            P(None, "head", None),
            P(None, None, "head"),
        ),
        check_vma=False,
    )
```

```python
import jax
import jax.numpy as jnp
from jax import lax
from jax.experimental import pallas as pl
from jax.experimental.pallas import tpu as pltpu
from jax.sharding import PartitionSpec as P

MESH = pl.DeviceIdType.MESH
F32 = jnp.float32
BF16 = jnp.bfloat16
T = 128
W = 320
D = 64
R = 64
ORDER = (0, 1, 2, 8, 5, 6, 7, 3, 4)
CHIPS = 32


def mm(a, b):
    return lax.dot_general(a, b, (((1,), (0,)), ((), ())), preferred_element_type=F32)


def mm_nt(a, b):
    return lax.dot_general(a, b, (((1,), (1,)), ((), ())), preferred_element_type=F32)


def kernel(
    adj_ref, x_hbm, og_hbm, wqkv_hbm, wo_hbm, down_hbm, up_hbm,
    lo_ref, gi_ref, ga_ref, gb_ref,
    wqkv, wo, down, up, wsem,
    xt, ogt, upt, downn, xsend, xrecv, ogsend, ogrecv,
    kvo, qgo, kvm, qgm, kvmsems, qgmsems, adjq, adjsems, stm, stmsems, ret, retbuf, retsems,
    aqm, agm, akm, avm, wq, wk, estm, om, invm, delm, dqm, dkm, dvm,
    kv, qg, kvsend, kvrecv, kvbsend, kvbrecv, qgsend, qgrecv, qgbsend, qgbrecv,
    st, stsend, strecv,
    a4q, a4g, a4kv, wtab, est4, o4acc, inv4, del4, dq4, dkv4,
    att, gs, low, inacc, losrc, lobuf, losend, lorecv,
    gisrc, gibuf, gisend, girecv, lgall, *parts,
):
    view = lax.axis_index("view")
    head = lax.axis_index("head")
    chip = view // 2
    core = lax.rem(view, 2)
    z = view // 8
    y = lax.rem(chip, 4)
    spot = lax.rem(view, 8)
    sgn = 2 * core - 1

    def at(c, k):
        return (lax.rem(c + 2 * CHIPS, CHIPS) * 2 + k, head)

    def step(p, side):
        near = ((p + 1) // 2) * (2 * lax.rem(p, 2) - 1)
        if isinstance(p, int):
            return {7: 4 * side, 8: -4 * side}.get(p, near)
        return jnp.where(p == 7, 4 * side, jnp.where(p == 8, -4 * side, near))

    sibling = (chip * 2 + 1 - core, head)

    def z_peer(o):
        return (lax.rem(z + o, 8) * 8 + spot, head)

    def spot_peer(o):
        return (z * 8 + lax.rem(spot + o, 8), head)

    def x_peer(o):
        return (view, lax.rem(head + o, 4))

    def remote(src, dst, ss, rs, dev):
        return pltpu.make_async_remote_copy(
            src_ref=src, dst_ref=dst, send_sem=ss, recv_sem=rs,
            device_id=dev, device_id_type=MESH,
        )

    mine = pl.ds(pl.multiple_of(head * W, 64), W)
    loads = [
        pltpu.make_async_copy(s, d, wsem.at[i])
        for i, (s, d) in enumerate(
            (
                (x_hbm.at[0], xt.at[mine]), (down_hbm, down), (up_hbm, up), (wqkv_hbm, wqkv),
                (og_hbm.at[0], ogt.at[mine]), (wo_hbm, wo),
            )
        )
    ]
    for load in loads:
        load.start()

    barrier = pltpu.get_barrier_semaphore()

    def greet(dev):
        pl.semaphore_signal(barrier, inc=1, device_id=dev, device_id_type=MESH)

    for o in (1, 2, 3):
        greet(x_peer(o))

    @pl.loop(1, 9)
    def _(o):
        greet((lax.rem(view + o, 64), head))
        greet((lax.rem(view + 64 - o, 64), head))

    for o in (2, 3, 4, 5, 6):
        greet(z_peer(o))
    pl.semaphore_wait(barrier, 24)

    def x_copy(o):
        return remote(x_hbm.at[0], xt.at[mine], xsend.at[o], xrecv.at[o], x_peer(o))

    def og_copy(o):
        return remote(og_hbm.at[0], ogt.at[mine], ogsend.at[o], ogrecv.at[o], x_peer(o))

    for o in (1, 3, 2):
        x_copy(o).start()

    adj = adj_ref[...].astype(F32)
    lane64 = lax.broadcasted_iota(jnp.int32, (1, 64), 1)

    def weight_of(v):
        one = jnp.sum(jnp.where(lane64 == v, adj, 0.0), axis=1, keepdims=True)
        return jnp.broadcast_to(one, (1, T))

    for p in range(9):
        c = lax.rem(chip + step(p, sgn) + 2 * CHIPS, CHIPS) * 2
        wtab[p : p + 1, 0:T] = weight_of(c + core)
        wtab[p : p + 1, T : 2 * T] = weight_of(c + 1 - core)
    lane = lax.broadcasted_iota(jnp.int32, (T, T), 1)
    left = lane < D

    def column(o):
        return (z * 8 + lax.rem(y + o, 4) * 2 + core, head)

    row = jnp.concatenate([adj, jnp.zeros((1, 64), F32)], axis=1)
    adjq[y] = jnp.broadcast_to(row, (8, T))

    def adj_copy(o):
        return remote(adjq.at[y], adjq.at[y], adjsems.at[0, o], adjsems.at[1, o], column(o))

    for o in (1, 3, 2):
        adj_copy(o).start()

    for load in loads[1:3]:
        load.wait()
    for m in range(3):
        upt[m] = jnp.transpose(up[R * m : R * (m + 1), :])
    for h in range(10):
        downn[T * h : T * (h + 1), :] = jnp.transpose(down[:, T * h : T * (h + 1)])

    loads[3].wait()
    loads[0].wait()
    for o in (1, 2, 3):
        x_copy(o).wait_recv()
    for o in (1, 3, 2):
        og_copy(o).start()
    low[...] = mm(down[...], xt[...]).astype(BF16)

    def project(m):
        main = mm(wqkv[W * m : W * (m + 1), :], xt[...])
        return (main + 0.5 * mm(upt[m], low[R * m : R * (m + 1), :])).astype(BF16)

    def lay_out(out, buf, first, second):
        for h in range(5):
            part = slice(D * h, D * (h + 1))
            tile = jnp.transpose(jnp.concatenate([first[part], second[part]], axis=0))
            if h < 4:
                out[h] = tile
            else:
                buf[0:T, :] = tile

    lay_out(kvo, kv, project(1), project(2))

    def pair_rows(p):
        return pl.ds(pl.multiple_of(p * 256, 256), T)

    def sib_rows(p):
        return pl.ds(pl.multiple_of(p * 256 + T, T), T)

    def sib_copy(buf, ss, rs, p, into):
        return remote(
            buf.at[pair_rows(p)], buf.at[sib_rows(into)], ss.at[into], rs.at[into], sibling
        )

    class Blocks:
        def __init__(self, buf, ss, rs, bs, br):
            self.buf, self.ss, self.rs, self.bs, self.br = buf, ss, rs, bs, br

        def copy(self, p):
            return remote(
                self.buf.at[0:T], self.buf.at[pair_rows(p)], self.ss.at[p], self.rs.at[p],
                at(chip - step(p, sgn), core),
            )

        def start_own(self):
            self.sib(0).start()
            for p in ORDER[1:]:
                self.copy(p).start()

        def sib(self, p):
            return sib_copy(self.buf, self.bs, self.br, p, 7 if p == 8 else p)

        def arrive(self, *ps):
            for p in ps:
                self.copy(p).wait_recv()
                if p != 7:
                    self.sib(p).start()

        def sib_arrived(self, p):
            if p != 8:
                self.sib(8 if p == 7 else p).wait_recv()

        def drain(self):
            for p in range(9):
                if p > 0:
                    self.copy(p).wait_send()
                if p != 7:
                    self.sib(p).wait_send()

    def span(group):
        return slice(512 * group, 512 * (group + 1))

    class Planes:
        def __init__(self, out, buf, sems):
            self.out, self.buf, self.sems = out, buf, sems

        def swap(self, o):
            return remote(
                self.out.at[lax.rem(y + o, 4)], self.buf.at[pl.ds(pl.multiple_of(y * T, T), T)],
                self.sems.at[0, o], self.sems.at[1, o], column(o),
            )

        def group(self, src, into, dev):
            return remote(
                self.buf.at[span(src)], self.buf.at[span(into)],
                self.sems.at[0, 4 + into], self.sems.at[1, 4 + into], dev,
            )

        def move(self, into):
            if into in (2, 4):
                return self.group(0, into, z_peer(1 if into == 2 else 7))
            return self.group(into - 1, into, sibling)

        def start(self):
            for o in (1, 3, 2):
                self.swap(o).start()
            self.buf[pl.ds(pl.multiple_of(y * T, T), T), :] = self.out[y]

        def swapped(self):
            for o in (1, 3, 2):
                self.swap(o).wait_recv()
            for g in (2, 4, 1):
                self.move(g).start()

        def arrive(self, group):
            self.move(group).wait_recv()
            if group in (2, 4):
                self.move(group + 1).start()

        def drain(self):
            for o in (1, 2, 3):
                self.swap(o).wait_send()
            for g in range(1, 6):
                self.move(g).wait_send()

    plane_keys = Planes(kvo, kvm, kvmsems)
    plane_queries = Planes(qgo, qgm, qgmsems)
    keys = Blocks(kv, kvsend, kvrecv, kvbsend, kvbrecv)
    queries = Blocks(qg, qgsend, qgrecv, qgbsend, qgbrecv)
    plane_keys.start()
    query = project(0)
    plane_keys.swapped()
    keys.start_own()
    loads[5].wait()
    loads[4].wait()
    for o in (1, 2, 3):
        og_copy(o).wait_recv()
    lay_out(qgo, qg, query, mm(wo[...], ogt[...]).astype(BF16))
    plane_queries.start()

    for o in (1, 2, 3):
        adj_copy(o).wait_recv()
    rows4 = jnp.concatenate([adjq[i, 0:1, :] for i in range(4)], axis=0)
    lane4 = lax.broadcasted_iota(jnp.int32, (4, T), 1)
    sub4 = lax.broadcasted_iota(jnp.int32, (4, T), 0)

    def view_of(group, i):
        plane = lax.rem(z + (0, 7, 1)[group // 2], 8)
        return plane * 8 + 2 * i + (core if group % 2 == 0 else 1 - core)

    for g in range(6):
        for i in range(4):
            one = jnp.sum(jnp.where(lane4 == view_of(g, i), rows4, 0.0), axis=1, keepdims=True)
            wq[2 * g + i // 2, 0:4, T * (i % 2) : T * (i % 2 + 1)] = jnp.broadcast_to(one, (4, T))

    plane_queries.swapped()
    queries.start_own()

    def tall(a, n):
        return jnp.concatenate([a] * n, axis=0)

    eighth = jnp.asarray(0.125, BF16)
    tile = qg[0:T, :]
    a4q[...] = jnp.where(left, tile * eighth, jnp.zeros_like(tile))
    a4g[...] = jnp.where(left, jnp.zeros_like(tile), tile)
    tile = kv[0:T, :]
    a4kv[0:T, :] = jnp.where(left, tile * eighth, jnp.zeros_like(tile))
    a4kv[T : 2 * T, :] = jnp.where(left, jnp.zeros_like(tile), tile)
    for i in range(4):
        part = slice(T * i, T * (i + 1))
        tile = qgm[part, :]
        aqm[part, :] = jnp.where(left, tile * eighth, jnp.zeros_like(tile))
        agm[part, :] = jnp.where(left, jnp.zeros_like(tile), tile)
        tile = kvm[part, :]
        akm[part, :] = jnp.where(left, tile * eighth, jnp.zeros_like(tile))
        avm[part, :] = jnp.where(left, jnp.zeros_like(tile), tile)

    for ref in (om, dqm, dkm, dvm, o4acc, dq4, dkv4):
        ref[...] = jnp.zeros_like(ref)

    def block(buf, p, n):
        return buf[pl.ds(pl.multiple_of(p * 256, 256), n), :]

    def forward(p, n):
        kv4 = block(kv, p, n)
        weight = wtab[pl.ds(p, 1), 0:n]
        ones = jnp.ones((n, T), BF16)
        e = jnp.where(weight > 0.0, jnp.exp(mm_nt(a4q[...], kv4)), 0.0).astype(BF16)
        est4[p, :, 0:n] = e
        o4acc[...] += mm(e, jnp.concatenate([kv4, ones], axis=1))

    def masked(weights, e):
        parts = [
            jnp.where(weights[i : i + 1, :] > 0.0, e[T * i : T * (i + 1)], 0.0) for i in range(4)
        ]
        return jnp.concatenate(parts, axis=0)

    def forward_plane(t):
        tile = block(kvm, t, 256)
        e = masked(wq[t], jnp.exp(mm_nt(aqm[...], tile))).astype(BF16)
        estm[t] = e
        om[...] += mm(e, jnp.concatenate([tile, jnp.ones((256, T), BF16)], axis=1))

    def run(work, blocks, order):
        for p in order:
            if blocks is not None:
                blocks.sib_arrived(p)
            work(p, T if p == 8 else 256)

    def run_plane(work, *groups):
        for g in groups:
            pl.loop(2 * g, 2 * g + 2)(work)

    run_plane(forward_plane, 0)
    plane_keys.arrive(2)
    plane_keys.arrive(4)
    plane_keys.arrive(1)
    run_plane(forward_plane, 1, 2, 4)
    for p in ORDER[1:]:
        keys.arrive(p)
    plane_keys.arrive(3)
    plane_keys.arrive(5)
    run_plane(forward_plane, 3, 5)
    run(forward, keys, ORDER)

    def put(stats, i, column):
        return jnp.where(lane == i, column, stats)

    stats = jnp.zeros((T, T), F32)
    invm[...] = 1.0 / om[:, T : 2 * T]
    attm = []
    for i in range(4):
        part = slice(T * i, T * (i + 1))
        own = (om[part, 0:T] * invm[part, :]).astype(BF16)
        attm.append(own)
        prod = own.astype(F32) * qgm[part, :].astype(F32)
        delta = jnp.sum(jnp.where(left, 0.0, prod), axis=1, keepdims=True)
        delm[part, :] = jnp.broadcast_to(delta, (T, T))
        stats = put(stats, i, invm[part, :])
        stats = put(stats, 4 + i, delta)
    inv = 1.0 / o4acc[:, T : 2 * T]
    inv4[...] = inv
    last = (o4acc[:, 0:T] * inv).astype(BF16)
    att[:, 256:320] = last[:, D:T]
    prod = last.astype(F32) * qg[0:T, :].astype(F32)
    delta = jnp.sum(jnp.where(left, 0.0, prod), axis=1, keepdims=True)
    del4[...] = jnp.broadcast_to(delta, (T, T))
    stats = put(stats, 16, inv)
    stats = put(stats, 17, delta)
    stats = jnp.transpose(stats)
    stm[0, 0:8, :] = stats[0:8, :]
    stm[0, 8:16, :] = jnp.concatenate([rows4, rows4], axis=0)
    st[0, 0] = stats[16:32, :]
    st[0, 0, 10:11, :] = row

    def stm_copy(i):
        dev, src, into = (
            (sibling, 0, slice(1, 2)), (z_peer(1), 0, slice(2, 4)), (z_peer(7), 0, slice(4, 6))
        )[i]
        src = slice(0, into.stop - into.start)
        return remote(stm.at[src], stm.at[into], stmsems.at[0, i], stmsems.at[1, i], dev)

    def stb_copy():
        return remote(st.at[0, 0], st.at[0, 1], stsend.at[0], strecv.at[0], sibling)

    def st_copy(p):
        return remote(
            st.at[0], st.at[p], stsend.at[p], strecv.at[p], at(chip - step(p, sgn), core)
        )

    stm_copy(0).start()
    stb_copy().start()

    def wide(a, n):
        return a if n == T else jnp.concatenate([a, a], axis=1)

    def backward_q(p, n):
        kv4 = block(kv, p, n)
        prob = est4[p, :, 0:n].astype(F32) * wide(inv4[...], n)
        dl = prob * (mm_nt(a4g[...], kv4) - wide(del4[...], n))
        dq4[...] += mm(dl.astype(BF16), kv4)

    def backward_q_plane(t):
        tile = block(kvm, t, 256)
        prob = estm[t].astype(F32) * wide(invm[...], 256)
        dl = prob * (mm_nt(agm[...], tile) - wide(delm[...], 256))
        dqm[...] += mm(dl.astype(BF16), tile)

    run_plane(backward_q_plane, 0)
    stm_copy(0).wait_recv()
    for i in (1, 2):
        stm_copy(i).start()
    run_plane(backward_q_plane, 1)
    stb_copy().wait_recv()
    for p in ORDER[1:]:
        st_copy(p).start()
    run_plane(backward_q_plane, 2, 3, 4, 5)

    def ret_copy(k, o):
        return remote(
            ret.at[k, lax.rem(y + o, 4)], retbuf.at[k, y],
            retsems.at[0, k, o], retsems.at[1, k, o], column(o),
        )

    def give_back(k, parts):
        for i in range(4):
            ret[k, i] = parts[i]
        for o in (1, 3, 2):
            ret_copy(k, o).start()
        retbuf[k, y] = ret[k, y]

    def given_back(k):
        for o in (1, 2, 3):
            ret_copy(k, o).wait_recv()

    give_back(
        0,
        [
            jnp.where(left, dqm[T * i : T * (i + 1), :] * 0.125, attm[i].astype(F32)).astype(BF16)
            for i in range(4)
        ],
    )
    run(backward_q, None, ORDER)
    gs[0, :, 256:320] = (dq4[:, 0:D] * 0.125).astype(BF16)
    plane_queries.arrive(2)
    plane_queries.arrive(4)
    plane_queries.arrive(1)
    for p in ORDER[1:]:
        queries.arrive(p)
    class Adapters:
        def __init__(self, which, lgsrc, lgbuf, acc, accb, rsbuf, zbuf, fin, sems):
            self.which, self.lgsrc, self.lgbuf = which, lgsrc, lgbuf
            self.acc, self.accb, self.rsbuf, self.zbuf, self.fin = acc, accb, rsbuf, zbuf, fin
            self.sems = sems
            self.count = R * len(which)
            self.share = self.count // 4

        def part(self, i):
            return pl.ds(pl.multiple_of(i * self.share, 16), self.share)

        def copies(self, stage):
            def copy(o):
                ends = {
                    0: lambda: (self.lgsrc, self.lgbuf.at[o], x_peer(o)),
                    1: lambda: (
                        self.accb.at[self.part(lax.rem(spot + o, 8))], self.rsbuf.at[o], spot_peer(o)
                    ),
                    2: lambda: (self.zbuf.at[z], self.zbuf.at[z], z_peer(o)),
                    3: lambda: (self.fin.at[spot], self.fin.at[spot], spot_peer(o)),
                }
                src, dst, dev = ends[stage]()
                return remote(src, dst, self.sems.at[stage, 0, o], self.sems.at[stage, 1, o], dev)

            return [copy(o) for o in range(1, 8 if stage else 4)]

        def start(self, stage):
            for c in self.copies(stage):
                c.start()

        def wait(self, stage):
            for c in self.copies(stage):
                c.wait_recv()

        def send_low(self):
            for i, m in enumerate(self.which):
                one = 0.5 * mm_nt(up[R * m : R * (m + 1), :], gs[m])
                self.lgsrc[R * i : R * (i + 1), :] = one.astype(BF16)
            self.start(0)
            for i, m in enumerate(self.which):
                self.acc[self.count + R * i : self.count + R * (i + 1), :] = 0.5 * mm(
                    low[R * m : R * (m + 1), :], gs[m]
                )

        def send_plane(self):
            self.wait(0)
            lg = self.lgsrc[...].astype(F32)
            for o in (1, 2, 3):
                lg = lg + self.lgbuf[o].astype(F32)
            lg = lg.astype(BF16)
            lgall[R * self.which[0] : R * self.which[0] + self.count, :] = lg
            self.acc[0 : self.count, :] = mm_nt(lg, xt[mine, :])
            self.accb[...] = self.acc[...].astype(BF16)
            self.start(1)

        def send_z(self):
            self.wait(1)
            total = self.acc[self.part(spot), :]
            for o in range(1, 8):
                total = total + self.rsbuf[o].astype(F32)
            self.zbuf[z] = total.astype(BF16)
            self.start(2)

        def send_back(self):
            self.wait(2)
            total = self.zbuf[0].astype(F32)
            for i in range(1, 8):
                total = total + self.zbuf[i].astype(F32)
            self.fin[spot] = total.astype(BF16)
            self.start(3)

        def finish(self):
            self.wait(3)
            for i in range(8):
                for r in range(0, self.share, 16):
                    which, at_row = divmod((i % 4) * self.share + r, R)
                    out = ga_ref if i < 4 else gb_ref
                    rows = slice(at_row, at_row + 16)
                    out[self.which[which], rows, :] = self.fin[i, r : r + 16, :].astype(F32)

        def drain(self):
            for stage in range(4):
                for c in self.copies(stage):
                    c.wait_send()

    late = Adapters((0, 1, 2), *parts)

    me_lane = lax.broadcasted_iota(jnp.int32, (1, T), 1) == view

    def backward_kv(p, n):
        qg4 = block(qg, p, n)
        sides = [st[p, s] for s in range(n // T)]
        w = [jnp.sum(jnp.where(me_lane, s[10:11, :], 0.0), axis=1, keepdims=True) for s in sides]
        w = [jnp.broadcast_to(one, (1, T)) for one in w]
        w = w[0] if n == T else jnp.concatenate(w, axis=1)
        sides = sides[0] if n == T else jnp.concatenate(sides, axis=1)
        both = mm_nt(a4kv[...], qg4)
        prob = jnp.where(w > 0.0, jnp.exp(both[0:T]) * sides[0:1, :], 0.0)
        dl = prob * (both[T : 2 * T] - sides[1:2, :])
        dkv4[...] += mm(jnp.concatenate([dl, prob], axis=0).astype(BF16), qg4)

    mine4 = z * 8 + 2 * sub4 + core

    def mask_kv(g):
        for i in range(4):
            line = jnp.broadcast_to(stm[g, 8 + i : 9 + i, :], (4, T))
            one = jnp.sum(jnp.where(lane4 == mine4, line, 0.0), axis=1, keepdims=True)
            wk[2 * g + i // 2, 0:4, T * (i % 2) : T * (i % 2 + 1)] = jnp.broadcast_to(one, (4, T))

    def backward_kv_plane(g):
        mask_kv(g)
        for half in range(2):
            t = 2 * g + half
            tile = block(qgm, t, 256)
            i = 2 * half
            inv = jnp.concatenate([stm[g, i : i + 1, :], stm[g, i + 1 : i + 2, :]], axis=1)
            delta = jnp.concatenate([stm[g, 4 + i : 5 + i, :], stm[g, 5 + i : 6 + i, :]], axis=1)
            prob = masked(wk[t], jnp.exp(mm_nt(akm[...], tile)) * inv)
            dl = prob * (mm_nt(avm[...], tile) - delta)
            dkm[...] += mm(dl.astype(BF16), tile)
            dvm[...] += mm(prob.astype(BF16), tile)

    def run_kv(*order):
        for p in order:
            if p != 0:
                st_copy(p).wait_recv()
        run(backward_kv, queries, order)

    backward_kv_plane(0)
    backward_kv_plane(1)
    for i in (1, 2):
        stm_copy(i).wait_recv()
    backward_kv_plane(2)
    backward_kv_plane(4)
    plane_queries.arrive(3)
    plane_queries.arrive(5)
    backward_kv_plane(3)
    backward_kv_plane(5)
    give_back(
        1,
        [
            jnp.where(left, dkm[T * i : T * (i + 1), :] * 0.125, dvm[T * i : T * (i + 1), :]).astype(
                BF16
            )
            for i in range(4)
        ],
    )
    run_kv(*ORDER)
    given_back(0)
    for h in range(4):
        gs[0, :, D * h : D * (h + 1)] = retbuf[0, h, :, 0:D]
        att[:, D * h : D * (h + 1)] = retbuf[0, h, :, D:T]

    inacc[...] = mm(gs[0], wqkv[0:W, :])
    gs[1, :, 256:320] = (dkv4[0:T, 0:D] * 0.125).astype(BF16)
    gs[2, :, 256:320] = dkv4[T : 2 * T, D:T].astype(BF16)
    given_back(1)
    for h in range(4):
        gs[1, :, D * h : D * (h + 1)] = retbuf[1, h, :, 0:D]
        gs[2, :, D * h : D * (h + 1)] = retbuf[1, h, :, D:T]

    late.send_low()

    share = inacc[...] + mm(gs[1], wqkv[W : 2 * W, :]) + mm(gs[2], wqkv[2 * W : 3 * W, :])
    share = share.astype(BF16)
    for h in range(4):
        gisrc[h] = share[:, W * h : W * (h + 1)]

    def gi_copy(o):
        return remote(
            gisrc.at[lax.rem(head + o, 4)], gibuf.at[o], gisend.at[o], girecv.at[o], x_peer(o)
        )

    for o in (1, 2, 3):
        gi_copy(o).start()

    share = mm(att[...], wo[...]).astype(BF16)
    for h in range(4):
        losrc[h] = share[:, W * h : W * (h + 1)]

    def lo_copy(o):
        return remote(
            losrc.at[lax.rem(head + o, 4)], lobuf.at[o], losend.at[o], lorecv.at[o], x_peer(o)
        )

    for o in (1, 2, 3):
        lo_copy(o).start()
    late.send_plane()

    late.send_z()

    own = gisrc[head].astype(F32)
    for o in (1, 2, 3):
        gi_copy(o).wait_recv()
        own = own + gibuf[o].astype(F32)
    gi_ref[0] = (jnp.transpose(own) + mm(downn[mine, :], lgall[...])).astype(BF16)
    out = losrc[head].astype(F32)
    for o in (1, 2, 3):
        lo_copy(o).wait_recv()
        out = out + lobuf[o].astype(F32)
    lo_ref[0] = jnp.transpose(out).astype(BF16)

    late.send_back()
    late.finish()

    for o in (1, 2, 3):
        x_copy(o).wait_send()
        og_copy(o).wait_send()
        lo_copy(o).wait_send()
        gi_copy(o).wait_send()
    keys.drain()
    queries.drain()
    plane_keys.drain()
    plane_queries.drain()
    for o in (1, 2, 3):
        adj_copy(o).wait_send()
        ret_copy(0, o).wait_send()
        ret_copy(1, o).wait_send()
    for i in range(3):
        stm_copy(i).wait_send()

    stb_copy().wait_send()
    for p in ORDER[1:]:
        st_copy(p).wait_send()
    late.drain()


def hand_over(*refs):
    source, target, held, sem = refs[0:4], refs[4:8], refs[8:12], refs[12]
    into = [pltpu.make_async_copy(s, h, sem.at[0, i]) for i, (s, h) in enumerate(zip(source, held))]
    out = [pltpu.make_async_copy(h, t, sem.at[1, i]) for i, (h, t) in enumerate(zip(held, target))]
    for copy in into:
        copy.start()
    for first, second in zip(into, out):
        first.wait()
        second.start()
    for copy in out:
        copy.wait()


def body(inputs, output_gradient, wqkv, wo, down, up, adjacent):
    vmem = pltpu.VMEM
    dma = pltpu.SemaphoreType.DMA
    scratch = [
        vmem((3 * W, 1280), BF16), vmem((W, 1280), BF16), vmem((3 * R, 1280), BF16),
        vmem((3 * R, W), BF16), dma((6,)),
        vmem((1280, T), BF16), vmem((1280, T), BF16), vmem((3, W, R), BF16),
        vmem((1280, 3 * R), BF16), dma((4,)), dma((4,)), dma((4,)), dma((4,)),
        vmem((4, T, T), BF16), vmem((4, T, T), BF16), vmem((24 * T, T), BF16),
        vmem((24 * T, T), BF16), dma((2, 10)), dma((2, 10)), vmem((4, 8, T), F32), dma((2, 4)),
        vmem((6, 16, T), F32), dma((2, 3)), vmem((2, 4, T, T), BF16), vmem((2, 4, T, T), BF16),
        dma((2, 2, 4)),
        vmem((512, T), BF16), vmem((512, T), BF16), vmem((512, T), BF16), vmem((512, T), BF16),
        vmem((12, 8, 256), F32), vmem((12, 8, 256), F32), vmem((12, 512, 256), BF16),
        vmem((512, 256), F32), vmem((512, T), F32), vmem((512, T), F32), vmem((512, T), F32),
        vmem((512, T), F32), vmem((512, T), F32),
        vmem((17 * T, T), BF16), vmem((17 * T, T), BF16),
        dma((9,)), dma((9,)), dma((8,)), dma((8,)), dma((9,)), dma((9,)), dma((8,)), dma((8,)),
        vmem((9, 2, 16, T), F32), dma((9,)), dma((9,)),
        vmem((T, T), BF16), vmem((T, T), BF16), vmem((256, T), BF16), vmem((16, 256), F32),
        vmem((9, T, 256), BF16), vmem((T, 256), F32), vmem((T, T), F32), vmem((T, T), F32),
        vmem((T, T), F32), vmem((256, T), F32),
        vmem((T, W), BF16), vmem((3, T, W), BF16), vmem((3 * R, T), BF16), vmem((T, 1280), F32),
        vmem((4, T, W), BF16), vmem((4, T, W), BF16), dma((4,)), dma((4,)),
        vmem((4, T, W), BF16), vmem((4, T, W), BF16), dma((4,)), dma((4,)), vmem((3 * R, T), BF16),
    ]
    share = vmem((8, 6 * R // 8, W), BF16)
    scratch += [vmem((3 * R, T), BF16), vmem((4, 3 * R, T), BF16), vmem((6 * R, W), F32)]
    scratch += [vmem((6 * R, W), BF16), share, share, share, dma((4, 2, 8))]
    whole = pl.BlockSpec(memory_space=pltpu.VMEM)
    hbm = pl.BlockSpec(memory_space=pltpu.HBM)
    results = pl.pallas_call(
        kernel,
        out_shape=(
            jax.ShapeDtypeStruct((1, W, T), BF16),
            jax.ShapeDtypeStruct((1, W, T), BF16),
            jax.ShapeDtypeStruct((3, R, W), F32),
            jax.ShapeDtypeStruct((3, R, W), F32),
        ),
        in_specs=[whole] + [hbm] * 6,
        out_specs=(whole,) * 4,
        scratch_shapes=scratch,
        compiler_params=pltpu.CompilerParams(
            collective_id=0, has_side_effects=True, vmem_limit_bytes=62 * 1024 * 1024
        ),
        name="layer",
    )(
        adjacent,
        jnp.swapaxes(inputs, 1, 2),
        jnp.swapaxes(output_gradient, 1, 2),
        jnp.swapaxes(wqkv, 1, 2).reshape(3 * W, 1280),
        wo,
        jnp.swapaxes(down, 1, 2).reshape(3 * R, 1280),
        up.reshape(3 * R, W),
    )
    layer_out, grad_inputs, grad_a, grad_b = pl.pallas_call(
        hand_over,
        out_shape=tuple(jax.ShapeDtypeStruct(r.shape, r.dtype) for r in results),
        in_specs=[hbm] * 4,
        out_specs=(hbm,) * 4,
        scratch_shapes=[vmem(r.shape, r.dtype) for r in results] + [dma((2, 4))],
        compiler_params=pltpu.CompilerParams(vmem_limit_bytes=62 * 1024 * 1024),
        name="hand_over",
    )(*results)
    return (
        jnp.swapaxes(layer_out, 1, 2),
        jnp.swapaxes(grad_inputs, 1, 2),
        jnp.swapaxes(grad_a, 1, 2),
        grad_b,
    )


def solution(mesh):
    return jax.shard_map(
        body,
        mesh=mesh,
        in_specs=(
            P("view", None, "head"),
            P("view", None, "head"),
            P(None, None, "head"),
            P("head", None),
            P(),
            P(None, None, "head"),
            P("view", None),
        ),
        out_specs=(
            P("view", None, "head"),
            P("view", None, "head"),
            P(None, "head", None),
            P(None, None, "head"),
        ),
        check_vma=False,
    )
```

```python
import jax
import jax.numpy as jnp
from jax import lax
from jax.experimental import pallas as pl
from jax.experimental.pallas import tpu as pltpu
from jax.sharding import PartitionSpec as P

MESH = pl.DeviceIdType.MESH
F32 = jnp.float32
BF16 = jnp.bfloat16
T = 128
W = 320
D = 64
R = 64
ORDER = (0, 1, 2, 8, 5, 6, 7, 3, 4)
CHIPS = 32


def mm(a, b):
    return lax.dot_general(a, b, (((1,), (0,)), ((), ())), preferred_element_type=F32)


def mm_nt(a, b):
    return lax.dot_general(a, b, (((1,), (1,)), ((), ())), preferred_element_type=F32)


def kernel(
    adj_ref, x_hbm, og_hbm, wqkv_hbm, wo_hbm, down_hbm, up_hbm,
    lo_ref, gi_ref, ga_ref, gb_ref,
    wqkv, wo, down, up, wsem,
    xt, ogt, upt, downn, xsend, xrecv, ogsend, ogrecv,
    kvo, qo, go, qsw, q4, kvosems, qosems, gosems, kvm, qgm, kvmsems, qgmsems, adjq, adjsems, stm, stmsems, ret, retbuf, retsems,
    aqm, agm, akm, avm, wq, wk, estm, om, invm, delm, dqm, dkm, dvm,
    kv, qg, kvsend, kvrecv, kvbsend, kvbrecv, qgsend, qgrecv, qgbsend, qgbrecv,
    st, stsend, strecv,
    a4q, a4g, a4kv, wtab, est4, o4acc, inv4, del4, dq4, dkv4,
    att, gs, low, inacc, losrc, lobuf, losend, lorecv,
    gisrc, gibuf, gisend, girecv, lgall, *parts,
):
    view = lax.axis_index("view")
    head = lax.axis_index("head")
    chip = view // 2
    core = lax.rem(view, 2)
    z = view // 8
    y = lax.rem(chip, 4)
    spot = lax.rem(view, 8)
    sgn = 2 * core - 1

    def at(c, k):
        return (lax.rem(c + 2 * CHIPS, CHIPS) * 2 + k, head)

    def step(p, side):
        near = ((p + 1) // 2) * (2 * lax.rem(p, 2) - 1)
        if isinstance(p, int):
            return {7: 4 * side, 8: -4 * side}.get(p, near)
        return jnp.where(p == 7, 4 * side, jnp.where(p == 8, -4 * side, near))

    sibling = (chip * 2 + 1 - core, head)

    def z_peer(o):
        return (lax.rem(z + o, 8) * 8 + spot, head)

    def x_peer(o):
        return (view, lax.rem(head + o, 4))

    def remote(src, dst, ss, rs, dev):
        return pltpu.make_async_remote_copy(
            src_ref=src, dst_ref=dst, send_sem=ss, recv_sem=rs,
            device_id=dev, device_id_type=MESH,
        )

    mine = pl.ds(pl.multiple_of(head * W, 64), W)
    loads = [
        pltpu.make_async_copy(s, d, wsem.at[i])
        for i, (s, d) in enumerate(
            (
                (x_hbm.at[0], xt.at[mine]), (down_hbm, down), (up_hbm, up), (wqkv_hbm, wqkv),
                (og_hbm.at[0], ogt.at[mine]), (wo_hbm, wo),
            )
        )
    ]
    loads[0].start()

    barrier = pltpu.get_barrier_semaphore()

    def greet(dev):
        pl.semaphore_signal(barrier, inc=1, device_id=dev, device_id_type=MESH)

    for o in (1, 2, 3):
        greet(x_peer(o))

    @pl.loop(1, 9)
    def _(o):
        greet((lax.rem(view + o, 64), head))
        greet((lax.rem(view + 64 - o, 64), head))

    for o in (2, 3, 4, 5, 6):
        greet(z_peer(o))
    pl.semaphore_wait(barrier, 24)

    def x_copy(o):
        return remote(x_hbm.at[0], xt.at[mine], xsend.at[o], xrecv.at[o], x_peer(o))

    def og_copy(o):
        return remote(og_hbm.at[0], ogt.at[mine], ogsend.at[o], ogrecv.at[o], x_peer(o))

    for o in (1, 3, 2):
        x_copy(o).start()
    for load in loads[1:]:
        load.start()

    adj = adj_ref[...].astype(F32)
    lane64 = lax.broadcasted_iota(jnp.int32, (1, 64), 1)

    def weight_of(v):
        one = jnp.sum(jnp.where(lane64 == v, adj, 0.0), axis=1, keepdims=True)
        return jnp.broadcast_to(one, (1, T))

    for p in range(9):
        c = lax.rem(chip + step(p, sgn) + 2 * CHIPS, CHIPS) * 2
        wtab[p : p + 1, 0:T] = weight_of(c + core)
        wtab[p : p + 1, T : 2 * T] = weight_of(c + 1 - core)
    lane = lax.broadcasted_iota(jnp.int32, (T, T), 1)
    left = lane < D

    def column(o):
        return (z * 8 + lax.rem(y + o, 4) * 2 + core, head)

    row = jnp.concatenate([adj, jnp.zeros((1, 64), F32)], axis=1)
    adjq[y] = jnp.broadcast_to(row, (8, T))

    def adj_copy(o):
        return remote(adjq.at[y], adjq.at[y], adjsems.at[0, o], adjsems.at[1, o], column(o))

    for o in (1, 3, 2):
        adj_copy(o).start()

    for load in loads[1:3]:
        load.wait()
    for m in range(3):
        upt[m] = jnp.transpose(up[R * m : R * (m + 1), :])
    for h in range(10):
        downn[T * h : T * (h + 1), :] = jnp.transpose(down[:, T * h : T * (h + 1)])

    loads[3].wait()
    loads[0].wait()
    for o in (1, 2, 3):
        x_copy(o).wait_recv()
    for o in (1, 3, 2):
        og_copy(o).start()
    low[...] = mm(down[...], xt[...]).astype(BF16)

    def project(m):
        main = mm(wqkv[W * m : W * (m + 1), :], xt[...])
        return (main + 0.5 * mm(upt[m], low[R * m : R * (m + 1), :])).astype(BF16)

    def lay_out(out, buf, first, second):
        for h in range(5):
            part = slice(D * h, D * (h + 1))
            tile = jnp.transpose(jnp.concatenate([first[part], second[part]], axis=0))
            if h < 4:
                out[h] = tile
            else:
                buf[0:T, :] = tile

    lay_out(kvo, kv, project(1), project(2))

    def pair_rows(p):
        return pl.ds(pl.multiple_of(p * 256, 256), T)

    def sib_rows(p):
        return pl.ds(pl.multiple_of(p * 256 + T, T), T)

    def sib_copy(buf, ss, rs, p, into):
        return remote(
            buf.at[pair_rows(p)], buf.at[sib_rows(into)], ss.at[into], rs.at[into], sibling
        )

    class Blocks:
        def __init__(self, buf, ss, rs, bs, br):
            self.buf, self.ss, self.rs, self.bs, self.br = buf, ss, rs, bs, br

        def copy(self, p):
            return remote(
                self.buf.at[0:T], self.buf.at[pair_rows(p)], self.ss.at[p], self.rs.at[p],
                at(chip - step(p, sgn), core),
            )

        def start_own(self):
            self.sib(0).start()
            for p in ORDER[1:]:
                self.copy(p).start()

        def sib(self, p):
            return sib_copy(self.buf, self.bs, self.br, p, 7 if p == 8 else p)

        def arrive(self, *ps):
            for p in ps:
                self.copy(p).wait_recv()
                if p != 7:
                    self.sib(p).start()

        def sib_arrived(self, p):
            if p != 8:
                self.sib(8 if p == 7 else p).wait_recv()

        def drain(self):
            for p in range(9):
                if p > 0:
                    self.copy(p).wait_send()
                if p != 7:
                    self.sib(p).wait_send()

    def span(group):
        return slice(512 * group, 512 * (group + 1))

    class Swap:
        def __init__(self, out, buf, sems):
            self.out, self.buf, self.sems = out, buf, sems
            self.rows = pl.ds(pl.multiple_of(y * T, T), T)

        def copy(self, o):
            return remote(
                self.out.at[lax.rem(y + o, 4)], self.buf.at[self.rows],
                self.sems.at[0, o], self.sems.at[1, o], column(o),
            )

        def start(self):
            for o in (1, 3, 2):
                self.copy(o).start()
            self.buf[self.rows, :] = self.out[y]

        def arrived(self):
            for o in (1, 3, 2):
                self.copy(o).wait_recv()

        def drain(self):
            for o in (1, 2, 3):
                self.copy(o).wait_send()

    class Planes:
        def __init__(self, buf, sems):
            self.buf, self.sems = buf, sems

        def move(self, into):
            src, dev = into - 1, sibling
            if into in (2, 4):
                src, dev = 0, z_peer(1 if into == 2 else 7)
            return remote(
                self.buf.at[span(src)], self.buf.at[span(into)],
                self.sems.at[0, into], self.sems.at[1, into], dev,
            )

        def start(self):
            for g in (2, 4, 1):
                self.move(g).start()

        def arrive(self, group):
            self.move(group).wait_recv()
            if group in (2, 4):
                self.move(group + 1).start()

        def drain(self):
            for g in range(1, 6):
                self.move(g).wait_send()

    swaps = [Swap(kvo, kvm, kvosems), Swap(qo, qsw, qosems), Swap(go, agm, gosems)]
    plane_keys = Planes(kvm, kvmsems)
    plane_queries = Planes(qgm, qgmsems)
    keys = Blocks(kv, kvsend, kvrecv, kvbsend, kvbrecv)
    queries = Blocks(qg, qgsend, qgrecv, qgbsend, qgbrecv)
    swaps[0].start()

    def spread(out, last, parts):
        for h in range(5):
            tile = jnp.transpose(jnp.concatenate(parts(slice(D * h, D * (h + 1))), axis=0))
            if h < 4:
                out[h] = tile
            else:
                last[...] = tile

    nothing = jnp.zeros((D, T), BF16)
    query = project(0)
    spread(qo, q4, lambda part: [query[part], nothing])
    swaps[1].start()
    swaps[0].arrived()
    plane_keys.start()
    keys.start_own()

    for o in (1, 2, 3):
        adj_copy(o).wait_recv()
    rows4 = jnp.concatenate([adjq[i, 0:1, :] for i in range(4)], axis=0)
    lane4 = lax.broadcasted_iota(jnp.int32, (4, T), 1)
    sub4 = lax.broadcasted_iota(jnp.int32, (4, T), 0)

    def view_of(group, i):
        plane = lax.rem(z + (0, 7, 1)[group // 2], 8)
        return plane * 8 + 2 * i + (core if group % 2 == 0 else 1 - core)

    for g in range(6):
        for i in range(4):
            one = jnp.sum(jnp.where(lane4 == view_of(g, i), rows4, 0.0), axis=1, keepdims=True)
            wq[2 * g + i // 2, 0:4, T * (i % 2) : T * (i % 2 + 1)] = jnp.broadcast_to(one, (4, T))

    eighth = jnp.asarray(0.125, BF16)
    swaps[1].arrived()
    a4q[...] = q4[...] * eighth
    tile = kv[0:T, :]
    a4kv[0:T, :] = jnp.where(left, tile * eighth, jnp.zeros_like(tile))
    a4kv[T : 2 * T, :] = jnp.where(left, jnp.zeros_like(tile), tile)
    quarters = [slice(T * i, T * (i + 1)) for i in range(4)]
    for part in quarters:
        aqm[part, :] = qsw[part, :] * eighth
        tile = kvm[part, :]
        akm[part, :] = jnp.where(left, tile * eighth, jnp.zeros_like(tile))
        avm[part, :] = jnp.where(left, jnp.zeros_like(tile), tile)

    loads[5].wait()
    loads[4].wait()
    for o in (1, 2, 3):
        og_copy(o).wait_recv()
    grad_att = mm(wo[...], ogt[...]).astype(BF16)
    spread(go, a4g, lambda part: [nothing, grad_att[part]])
    swaps[2].start()
    qg[0:T, :] = jnp.where(left, q4[...], a4g[...])

    for ref in (om, dqm, dkm, dvm, o4acc, dq4, dkv4):
        ref[...] = jnp.zeros_like(ref)

    def block(buf, p, n):
        return buf[pl.ds(pl.multiple_of(p * 256, 256), n), :]

    def forward(p, n):
        kv4 = block(kv, p, n)
        weight = wtab[pl.ds(p, 1), 0:n]
        ones = jnp.ones((n, T), BF16)
        e = jnp.where(weight > 0.0, jnp.exp(mm_nt(a4q[...], kv4)), 0.0).astype(BF16)
        est4[p, :, 0:n] = e
        o4acc[...] += mm(e, jnp.concatenate([kv4, ones], axis=1))

    def masked(weights, e):
        parts = [
            jnp.where(weights[i : i + 1, :] > 0.0, e[T * i : T * (i + 1)], 0.0) for i in range(4)
        ]
        return jnp.concatenate(parts, axis=0)

    def forward_plane(t):
        tile = block(kvm, t, 256)
        e = masked(wq[t], jnp.exp(mm_nt(aqm[...], tile))).astype(BF16)
        estm[t] = e
        om[...] += mm(e, jnp.concatenate([tile, jnp.ones((256, T), BF16)], axis=1))

    def run(work, blocks, order):
        for p in order:
            if blocks is not None:
                blocks.sib_arrived(p)
            work(p, T if p == 8 else 256)

    def run_plane(work, *groups):
        for g in groups:
            pl.loop(2 * g, 2 * g + 2)(work)

    run_plane(forward_plane, 0)
    swaps[2].arrived()
    for part in quarters:
        qgm[part, :] = jnp.where(left, qsw[part, :], agm[part, :])
    plane_queries.start()
    queries.start_own()
    plane_keys.arrive(2)
    plane_keys.arrive(4)
    plane_keys.arrive(1)
    run_plane(forward_plane, 1, 2, 4)
    for p in ORDER[1:]:
        keys.arrive(p)
    plane_keys.arrive(3)
    plane_keys.arrive(5)
    run_plane(forward_plane, 3, 5)
    run(forward, keys, ORDER)

    def put(stats, i, column):
        return jnp.where(lane == i, column, stats)

    stats = jnp.zeros((T, T), F32)
    invm[...] = 1.0 / om[:, T : 2 * T]
    attm = []
    for i in range(4):
        part = slice(T * i, T * (i + 1))
        own = (om[part, 0:T] * invm[part, :]).astype(BF16)
        attm.append(own)
        prod = own.astype(F32) * qgm[part, :].astype(F32)
        delta = jnp.sum(jnp.where(left, 0.0, prod), axis=1, keepdims=True)
        delm[part, :] = jnp.broadcast_to(delta, (T, T))
        stats = put(stats, i, invm[part, :])
        stats = put(stats, 4 + i, delta)
    inv = 1.0 / o4acc[:, T : 2 * T]
    inv4[...] = inv
    last = (o4acc[:, 0:T] * inv).astype(BF16)
    att[:, 256:320] = last[:, D:T]
    prod = last.astype(F32) * qg[0:T, :].astype(F32)
    delta = jnp.sum(jnp.where(left, 0.0, prod), axis=1, keepdims=True)
    del4[...] = jnp.broadcast_to(delta, (T, T))
    stats = put(stats, 16, inv)
    stats = put(stats, 17, delta)
    stats = jnp.transpose(stats)
    stm[0, 0:8, :] = stats[0:8, :]
    stm[0, 8:16, :] = jnp.concatenate([rows4, rows4], axis=0)
    st[0, 0] = stats[16:32, :]
    st[0, 0, 10:11, :] = row

    def stm_copy(i):
        dev, src, into = (
            (sibling, 0, slice(1, 2)), (z_peer(1), 0, slice(2, 4)), (z_peer(7), 0, slice(4, 6))
        )[i]
        src = slice(0, into.stop - into.start)
        return remote(stm.at[src], stm.at[into], stmsems.at[0, i], stmsems.at[1, i], dev)

    def stb_copy():
        return remote(st.at[0, 0], st.at[0, 1], stsend.at[0], strecv.at[0], sibling)

    def st_copy(p):
        return remote(
            st.at[0], st.at[p], stsend.at[p], strecv.at[p], at(chip - step(p, sgn), core)
        )

    stm_copy(0).start()
    stb_copy().start()

    def wide(a, n):
        return a if n == T else jnp.concatenate([a, a], axis=1)

    def backward_q(p, n):
        kv4 = block(kv, p, n)
        prob = est4[p, :, 0:n].astype(F32) * wide(inv4[...], n)
        dl = prob * (mm_nt(a4g[...], kv4) - wide(del4[...], n))
        dq4[...] += mm(dl.astype(BF16), kv4)

    def backward_q_plane(t):
        tile = block(kvm, t, 256)
        prob = estm[t].astype(F32) * wide(invm[...], 256)
        dl = prob * (mm_nt(agm[...], tile) - wide(delm[...], 256))
        dqm[...] += mm(dl.astype(BF16), tile)

    run_plane(backward_q_plane, 0)
    stm_copy(0).wait_recv()
    for i in (1, 2):
        stm_copy(i).start()
    run_plane(backward_q_plane, 1)
    stb_copy().wait_recv()
    for p in ORDER[1:]:
        st_copy(p).start()
    run_plane(backward_q_plane, 2, 3, 4, 5)

    def ret_copy(k, o):
        return remote(
            ret.at[k, lax.rem(y + o, 4)], retbuf.at[k, y],
            retsems.at[0, k, o], retsems.at[1, k, o], column(o),
        )

    def give_back(k, parts):
        for i in range(4):
            ret[k, i] = parts[i]
        for o in (1, 3, 2):
            ret_copy(k, o).start()
        retbuf[k, y] = ret[k, y]

    def given_back(k):
        for o in (1, 2, 3):
            ret_copy(k, o).wait_recv()

    give_back(
        0,
        [
            jnp.where(left, dqm[T * i : T * (i + 1), :] * 0.125, attm[i].astype(F32)).astype(BF16)
            for i in range(4)
        ],
    )
    run(backward_q, None, ORDER)
    gs[0, :, 256:320] = (dq4[:, 0:D] * 0.125).astype(BF16)
    plane_queries.arrive(2)
    plane_queries.arrive(4)
    plane_queries.arrive(1)
    for p in ORDER[1:]:
        queries.arrive(p)
    class Adapters:
        def __init__(
            self, which, lgsrc, lgbuf, acc, accb, other, half, halfb, rsbuf, zbuf, fin, sems
        ):
            self.which, self.lgsrc, self.lgbuf, self.acc, self.accb = which, lgsrc, lgbuf, acc, accb
            self.other, self.half, self.halfb = other, half, halfb
            self.rsbuf, self.zbuf, self.fin, self.sems = rsbuf, zbuf, fin, sems
            self.count = R * len(which)
            self.share = self.count // 4
            self.spot = core * 4 + y

        def part(self, i):
            return pl.ds(pl.multiple_of(i * self.share, 16), self.share)

        def core_rows(self, k):
            return pl.ds(pl.multiple_of(k * self.count, 64), self.count)

        def copies(self, stage):
            def copy(o):
                ends = {
                    0: lambda: (self.lgsrc, self.lgbuf.at[o], x_peer(o)),
                    1: lambda: (self.accb.at[self.core_rows(1 - core)], self.other, sibling),
                    2: lambda: (
                        self.halfb.at[self.part(lax.rem(y + o, 4))], self.rsbuf.at[o], column(o)
                    ),
                    3: lambda: (self.zbuf.at[z], self.zbuf.at[z], z_peer(o)),
                    4: lambda: (self.fin.at[self.spot], self.fin.at[self.spot], column(o)),
                    5: lambda: (
                        self.fin.at[pl.ds(4 * core, 4)], self.fin.at[pl.ds(4 * core, 4)], sibling
                    ),
                }
                src, dst, dev = ends[stage]()
                return remote(src, dst, self.sems.at[stage, 0, o], self.sems.at[stage, 1, o], dev)

            return [copy(o) for o in range(1, (4, 2, 4, 8, 4, 2)[stage])]

        def start(self, stage):
            for c in self.copies(stage):
                c.start()

        def wait(self, stage):
            for c in self.copies(stage):
                c.wait_recv()

        def send_low(self):
            for i, m in enumerate(self.which):
                one = 0.5 * mm_nt(up[R * m : R * (m + 1), :], gs[m])
                self.lgsrc[R * i : R * (i + 1), :] = one.astype(BF16)
            self.start(0)
            for i, m in enumerate(self.which):
                self.acc[self.count + R * i : self.count + R * (i + 1), :] = 0.5 * mm(
                    low[R * m : R * (m + 1), :], gs[m]
                )

        def send_plane(self):
            self.wait(0)
            lg = self.lgsrc[...].astype(F32)
            for o in (1, 2, 3):
                lg = lg + self.lgbuf[o].astype(F32)
            lg = lg.astype(BF16)
            lgall[R * self.which[0] : R * self.which[0] + self.count, :] = lg
            self.acc[0 : self.count, :] = mm_nt(lg, xt[mine, :])
            self.accb[...] = self.acc[...].astype(BF16)
            self.start(1)

        def send_column(self):
            self.wait(1)
            self.half[...] = self.acc[self.core_rows(core), :] + self.other[...].astype(F32)
            self.halfb[...] = self.half[...].astype(BF16)
            self.start(2)

        def send_z(self):
            self.wait(2)
            total = self.half[self.part(y), :]
            for o in range(1, 4):
                total = total + self.rsbuf[o].astype(F32)
            self.zbuf[z] = total.astype(BF16)
            self.start(3)

        def send_back(self):
            self.wait(3)
            total = self.zbuf[0].astype(F32)
            for i in range(1, 8):
                total = total + self.zbuf[i].astype(F32)
            self.fin[self.spot] = total.astype(BF16)
            self.start(4)

        def finish(self):
            self.wait(4)
            self.start(5)
            self.wait(5)
            for i in range(8):
                for r in range(0, self.share, 16):
                    which, at_row = divmod((i % 4) * self.share + r, R)
                    out = ga_ref if i < 4 else gb_ref
                    rows = slice(at_row, at_row + 16)
                    out[self.which[which], rows, :] = self.fin[i, r : r + 16, :].astype(F32)

        def drain(self):
            for stage in range(6):
                for c in self.copies(stage):
                    c.wait_send()

    early = Adapters((0,), *parts[:11])
    late = Adapters((1, 2), *parts[11:])

    me_lane = lax.broadcasted_iota(jnp.int32, (1, T), 1) == view

    def backward_kv(p, n):
        qg4 = block(qg, p, n)
        sides = [st[p, s] for s in range(n // T)]
        w = [jnp.sum(jnp.where(me_lane, s[10:11, :], 0.0), axis=1, keepdims=True) for s in sides]
        w = [jnp.broadcast_to(one, (1, T)) for one in w]
        w = w[0] if n == T else jnp.concatenate(w, axis=1)
        sides = sides[0] if n == T else jnp.concatenate(sides, axis=1)
        both = mm_nt(a4kv[...], qg4)
        prob = jnp.where(w > 0.0, jnp.exp(both[0:T]) * sides[0:1, :], 0.0)
        dl = prob * (both[T : 2 * T] - sides[1:2, :])
        dkv4[...] += mm(jnp.concatenate([dl, prob], axis=0).astype(BF16), qg4)

    mine4 = z * 8 + 2 * sub4 + core

    def mask_kv(g):
        for i in range(4):
            line = jnp.broadcast_to(stm[g, 8 + i : 9 + i, :], (4, T))
            one = jnp.sum(jnp.where(lane4 == mine4, line, 0.0), axis=1, keepdims=True)
            wk[2 * g + i // 2, 0:4, T * (i % 2) : T * (i % 2 + 1)] = jnp.broadcast_to(one, (4, T))

    def backward_kv_plane(g):
        mask_kv(g)
        for half in range(2):
            t = 2 * g + half
            tile = block(qgm, t, 256)
            i = 2 * half
            inv = jnp.concatenate([stm[g, i : i + 1, :], stm[g, i + 1 : i + 2, :]], axis=1)
            delta = jnp.concatenate([stm[g, 4 + i : 5 + i, :], stm[g, 5 + i : 6 + i, :]], axis=1)
            prob = masked(wk[t], jnp.exp(mm_nt(akm[...], tile)) * inv)
            dl = prob * (mm_nt(avm[...], tile) - delta)
            dkm[...] += mm(dl.astype(BF16), tile)
            dvm[...] += mm(prob.astype(BF16), tile)

    def run_kv(*order):
        for p in order:
            if p != 0:
                st_copy(p).wait_recv()
        run(backward_kv, queries, order)

    backward_kv_plane(0)
    backward_kv_plane(1)
    for i in (1, 2):
        stm_copy(i).wait_recv()
    backward_kv_plane(2)
    backward_kv_plane(4)
    plane_queries.arrive(3)
    plane_queries.arrive(5)
    backward_kv_plane(3)
    backward_kv_plane(5)
    give_back(
        1,
        [
            jnp.where(left, dkm[T * i : T * (i + 1), :] * 0.125, dvm[T * i : T * (i + 1), :]).astype(
                BF16
            )
            for i in range(4)
        ],
    )
    run_kv(*ORDER)
    given_back(0)
    for h in range(4):
        gs[0, :, D * h : D * (h + 1)] = retbuf[0, h, :, 0:D]
        att[:, D * h : D * (h + 1)] = retbuf[0, h, :, D:T]

    early.send_low()
    inacc[...] = mm(gs[0], wqkv[0:W, :])
    gs[1, :, 256:320] = (dkv4[0:T, 0:D] * 0.125).astype(BF16)
    gs[2, :, 256:320] = dkv4[T : 2 * T, D:T].astype(BF16)
    given_back(1)
    for h in range(4):
        gs[1, :, D * h : D * (h + 1)] = retbuf[1, h, :, 0:D]
        gs[2, :, D * h : D * (h + 1)] = retbuf[1, h, :, D:T]

    late.send_low()
    early.send_plane()

    share = inacc[...] + mm(gs[1], wqkv[W : 2 * W, :]) + mm(gs[2], wqkv[2 * W : 3 * W, :])
    share = share.astype(BF16)
    for h in range(4):
        gisrc[h] = share[:, W * h : W * (h + 1)]

    def gi_copy(o):
        return remote(
            gisrc.at[lax.rem(head + o, 4)], gibuf.at[o], gisend.at[o], girecv.at[o], x_peer(o)
        )

    for o in (1, 2, 3):
        gi_copy(o).start()

    share = mm(att[...], wo[...]).astype(BF16)
    for h in range(4):
        losrc[h] = share[:, W * h : W * (h + 1)]

    def lo_copy(o):
        return remote(
            losrc.at[lax.rem(head + o, 4)], lobuf.at[o], losend.at[o], lorecv.at[o], x_peer(o)
        )

    for o in (1, 2, 3):
        lo_copy(o).start()
    early.send_column()
    late.send_plane()
    early.send_z()
    late.send_column()
    late.send_z()

    own = gisrc[head].astype(F32)
    for o in (1, 2, 3):
        gi_copy(o).wait_recv()
        own = own + gibuf[o].astype(F32)
    gi_ref[0] = (jnp.transpose(own) + mm(downn[mine, :], lgall[...])).astype(BF16)
    out = losrc[head].astype(F32)
    for o in (1, 2, 3):
        lo_copy(o).wait_recv()
        out = out + lobuf[o].astype(F32)
    lo_ref[0] = jnp.transpose(out).astype(BF16)

    early.send_back()
    late.send_back()
    early.finish()
    late.finish()

    for o in (1, 2, 3):
        x_copy(o).wait_send()
        og_copy(o).wait_send()
        lo_copy(o).wait_send()
        gi_copy(o).wait_send()
    keys.drain()
    queries.drain()
    plane_keys.drain()
    plane_queries.drain()
    for swap in swaps:
        swap.drain()
    for o in (1, 2, 3):
        adj_copy(o).wait_send()
        ret_copy(0, o).wait_send()
        ret_copy(1, o).wait_send()
    for i in range(3):
        stm_copy(i).wait_send()

    stb_copy().wait_send()
    for p in ORDER[1:]:
        st_copy(p).wait_send()
    early.drain()
    late.drain()


def hand_over(*refs):
    source, target, held, sem = refs[0:4], refs[4:8], refs[8:12], refs[12]
    into = [pltpu.make_async_copy(s, h, sem.at[0, i]) for i, (s, h) in enumerate(zip(source, held))]
    out = [pltpu.make_async_copy(h, t, sem.at[1, i]) for i, (h, t) in enumerate(zip(held, target))]
    for copy in into:
        copy.start()
    for first, second in zip(into, out):
        first.wait()
        second.start()
    for copy in out:
        copy.wait()


def body(inputs, output_gradient, wqkv, wo, down, up, adjacent):
    vmem = pltpu.VMEM
    dma = pltpu.SemaphoreType.DMA
    scratch = [
        vmem((3 * W, 1280), BF16), vmem((W, 1280), BF16), vmem((3 * R, 1280), BF16),
        vmem((3 * R, W), BF16), dma((6,)),
        vmem((1280, T), BF16), vmem((1280, T), BF16), vmem((3, W, R), BF16),
        vmem((1280, 3 * R), BF16), dma((4,)), dma((4,)), dma((4,)), dma((4,)),
        vmem((4, T, T), BF16), vmem((4, T, T), BF16), vmem((4, T, T), BF16), vmem((512, T), BF16),
        vmem((T, T), BF16), dma((2, 4)), dma((2, 4)), dma((2, 4)), vmem((24 * T, T), BF16),
        vmem((24 * T, T), BF16), dma((2, 6)), dma((2, 6)), vmem((4, 8, T), F32), dma((2, 4)),
        vmem((6, 16, T), F32), dma((2, 3)), vmem((2, 4, T, T), BF16), vmem((2, 4, T, T), BF16),
        dma((2, 2, 4)),
        vmem((512, T), BF16), vmem((512, T), BF16), vmem((512, T), BF16), vmem((512, T), BF16),
        vmem((12, 8, 256), F32), vmem((12, 8, 256), F32), vmem((12, 512, 256), BF16),
        vmem((512, 256), F32), vmem((512, T), F32), vmem((512, T), F32), vmem((512, T), F32),
        vmem((512, T), F32), vmem((512, T), F32),
        vmem((17 * T, T), BF16), vmem((17 * T, T), BF16),
        dma((9,)), dma((9,)), dma((8,)), dma((8,)), dma((9,)), dma((9,)), dma((8,)), dma((8,)),
        vmem((9, 2, 16, T), F32), dma((9,)), dma((9,)),
        vmem((T, T), BF16), vmem((T, T), BF16), vmem((256, T), BF16), vmem((16, 256), F32),
        vmem((9, T, 256), BF16), vmem((T, 256), F32), vmem((T, T), F32), vmem((T, T), F32),
        vmem((T, T), F32), vmem((256, T), F32),
        vmem((T, W), BF16), vmem((3, T, W), BF16), vmem((3 * R, T), BF16), vmem((T, 1280), F32),
        vmem((4, T, W), BF16), vmem((4, T, W), BF16), dma((4,)), dma((4,)),
        vmem((4, T, W), BF16), vmem((4, T, W), BF16), dma((4,)), dma((4,)), vmem((3 * R, T), BF16),
    ]
    for count in (R, 2 * R):
        share, half = vmem((8, count // 4, W), BF16), vmem((count, W), BF16)
        scratch += [vmem((count, T), BF16), vmem((4, count, T), BF16), vmem((2 * count, W), F32)]
        scratch += [vmem((2 * count, W), BF16), half, vmem((count, W), F32), half]
        scratch += [share, share, share, dma((6, 2, 8))]
    whole = pl.BlockSpec(memory_space=pltpu.VMEM)
    hbm = pl.BlockSpec(memory_space=pltpu.HBM)
    results = pl.pallas_call(
        kernel,
        out_shape=(
            jax.ShapeDtypeStruct((1, W, T), BF16),
            jax.ShapeDtypeStruct((1, W, T), BF16),
            jax.ShapeDtypeStruct((3, R, W), F32),
            jax.ShapeDtypeStruct((3, R, W), F32),
        ),
        in_specs=[whole] + [hbm] * 6,
        out_specs=(whole,) * 4,
        scratch_shapes=scratch,
        compiler_params=pltpu.CompilerParams(
            collective_id=0, has_side_effects=True, vmem_limit_bytes=62 * 1024 * 1024
        ),
        name="layer",
    )(
        adjacent,
        jnp.swapaxes(inputs, 1, 2),
        jnp.swapaxes(output_gradient, 1, 2),
        jnp.swapaxes(wqkv, 1, 2).reshape(3 * W, 1280),
        wo,
        jnp.swapaxes(down, 1, 2).reshape(3 * R, 1280),
        up.reshape(3 * R, W),
    )
    layer_out, grad_inputs, grad_a, grad_b = pl.pallas_call(
        hand_over,
        out_shape=tuple(jax.ShapeDtypeStruct(r.shape, r.dtype) for r in results),
        in_specs=[hbm] * 4,
        out_specs=(hbm,) * 4,
        scratch_shapes=[vmem(r.shape, r.dtype) for r in results] + [dma((2, 4))],
        compiler_params=pltpu.CompilerParams(vmem_limit_bytes=62 * 1024 * 1024),
        name="hand_over",
    )(*results)
    return (
        jnp.swapaxes(layer_out, 1, 2),
        jnp.swapaxes(grad_inputs, 1, 2),
        jnp.swapaxes(grad_a, 1, 2),
        grad_b,
    )


def solution(mesh):
    return jax.shard_map(
        body,
        mesh=mesh,
        in_specs=(
            P("view", None, "head"),
            P("view", None, "head"),
            P(None, None, "head"),
            P("head", None),
            P(),
            P(None, None, "head"),
            P("view", None),
        ),
        out_specs=(
            P("view", None, "head"),
            P("view", None, "head"),
            P(None, "head", None),
            P(None, None, "head"),
        ),
        check_vma=False,
    )
```

```python
import jax
import jax.numpy as jnp
from jax import lax
from jax.experimental import pallas as pl
from jax.experimental.pallas import tpu as pltpu
from jax.sharding import PartitionSpec as P

MESH = pl.DeviceIdType.MESH
F32 = jnp.float32
BF16 = jnp.bfloat16
T = 128
W = 320
D = 64
R = 64
ORDER = (0, 3, 4, 1, 2, 5, 6, 8, 7)
CHIPS = 32


def mm(a, b):
    return lax.dot_general(a, b, (((1,), (0,)), ((), ())), preferred_element_type=F32)


def mm_nt(a, b):
    return lax.dot_general(a, b, (((1,), (1,)), ((), ())), preferred_element_type=F32)


def kernel(
    adj_ref, x_hbm, og_hbm, wqkv_hbm, wo_hbm, down_hbm, up_hbm,
    lo_ref, gi_ref, ga_ref, gb_ref,
    wqkv, wo, down, up, wsem,
    xt, ogt, upt, downn, xsend, xrecv, ogsend, ogrecv,
    kvo, qo, go, qsw, q4, kvosems, qosems, gosems, kvm, qgm, kvmsems, qgmsems, adjq, adjsems, stm, stmsems, ret, retbuf, retsems,
    aqm, agm, akm, avm, wq, wk, estm, om, invm, delm, dqm, dkm, dvm,
    kv, qg, kvsend, kvrecv, kvbsend, kvbrecv, qgsend, qgrecv, qgbsend, qgbrecv,
    st, stsend, strecv,
    a4q, a4g, a4kv, wtab, est4, o4acc, inv4, del4, dq4, dkv4,
    att, gs, low, inacc, losrc, lobuf, losend, lorecv,
    gisrc, gibuf, gisend, girecv, lgall, *parts,
):
    view = lax.axis_index("view")
    head = lax.axis_index("head")
    chip = view // 2
    core = lax.rem(view, 2)
    z = view // 8
    y = lax.rem(chip, 4)
    spot = lax.rem(view, 8)
    sgn = 2 * core - 1

    def at(c, k):
        return (lax.rem(c + 2 * CHIPS, CHIPS) * 2 + k, head)

    def step(p, side):
        near = ((p + 1) // 2) * (2 * lax.rem(p, 2) - 1)
        if isinstance(p, int):
            return {7: 4 * side, 8: -4 * side}.get(p, near)
        return jnp.where(p == 7, 4 * side, jnp.where(p == 8, -4 * side, near))

    sibling = (chip * 2 + 1 - core, head)

    def z_peer(o):
        return (lax.rem(z + o, 8) * 8 + spot, head)

    def x_peer(o):
        return (view, lax.rem(head + o, 4))

    def remote(src, dst, ss, rs, dev):
        return pltpu.make_async_remote_copy(
            src_ref=src, dst_ref=dst, send_sem=ss, recv_sem=rs,
            device_id=dev, device_id_type=MESH,
        )

    mine = pl.ds(pl.multiple_of(head * W, 64), W)
    loads = [
        pltpu.make_async_copy(s, d, wsem.at[i])
        for i, (s, d) in enumerate(
            (
                (x_hbm.at[0], xt.at[mine]), (down_hbm, down), (up_hbm, up), (wqkv_hbm, wqkv),
                (og_hbm.at[0], ogt.at[mine]), (wo_hbm, wo),
            )
        )
    ]
    loads[0].start()

    barrier = pltpu.get_barrier_semaphore()

    def greet(dev):
        pl.semaphore_signal(barrier, inc=1, device_id=dev, device_id_type=MESH)

    for o in (1, 2, 3):
        greet(x_peer(o))

    @pl.loop(1, 9)
    def _(o):
        greet((lax.rem(view + o, 64), head))
        greet((lax.rem(view + 64 - o, 64), head))

    for o in (2, 3, 4, 5, 6):
        greet(z_peer(o))
    pl.semaphore_wait(barrier, 24)

    def x_copy(o):
        return remote(x_hbm.at[0], xt.at[mine], xsend.at[o], xrecv.at[o], x_peer(o))

    def og_copy(o):
        return remote(og_hbm.at[0], ogt.at[mine], ogsend.at[o], ogrecv.at[o], x_peer(o))

    for o in (2, 1, 3):
        x_copy(o).start()
    for load in loads[1:]:
        load.start()

    adj = adj_ref[...].astype(F32)
    lane64 = lax.broadcasted_iota(jnp.int32, (1, 64), 1)

    def weight_of(v):
        one = jnp.sum(jnp.where(lane64 == v, adj, 0.0), axis=1, keepdims=True)
        return jnp.broadcast_to(one, (1, T))

    for p in range(9):
        c = lax.rem(chip + step(p, sgn) + 2 * CHIPS, CHIPS) * 2
        wtab[p : p + 1, 0:T] = weight_of(c + core)
        wtab[p : p + 1, T : 2 * T] = weight_of(c + 1 - core)
    lane = lax.broadcasted_iota(jnp.int32, (T, T), 1)
    left = lane < D

    def column(o):
        return (z * 8 + lax.rem(y + o, 4) * 2 + core, head)

    row = jnp.concatenate([adj, jnp.zeros((1, 64), F32)], axis=1)
    adjq[y] = jnp.broadcast_to(row, (8, T))

    def adj_copy(o):
        return remote(adjq.at[y], adjq.at[y], adjsems.at[0, o], adjsems.at[1, o], column(o))

    for o in (2, 1, 3):
        adj_copy(o).start()

    for load in loads[1:3]:
        load.wait()
    for m in range(3):
        upt[m] = jnp.transpose(up[R * m : R * (m + 1), :])
    for h in range(10):
        downn[T * h : T * (h + 1), :] = jnp.transpose(down[:, T * h : T * (h + 1)])

    loads[3].wait()
    loads[0].wait()
    for o in (1, 2, 3):
        x_copy(o).wait_recv()
    for o in (2, 1, 3):
        og_copy(o).start()
    low[...] = mm(down[...], xt[...]).astype(BF16)

    def project(m):
        main = mm(wqkv[W * m : W * (m + 1), :], xt[...])
        return (main + 0.5 * mm(upt[m], low[R * m : R * (m + 1), :])).astype(BF16)

    def lay_out(out, buf, first, second):
        for h in range(5):
            part = slice(D * h, D * (h + 1))
            tile = jnp.transpose(jnp.concatenate([first[part], second[part]], axis=0))
            if h < 4:
                out[h] = tile
            else:
                buf[0:T, :] = tile

    lay_out(kvo, kv, project(1), project(2))

    def pair_rows(p):
        return pl.ds(pl.multiple_of(p * 256, 256), T)

    def sib_rows(p):
        return pl.ds(pl.multiple_of(p * 256 + T, T), T)

    def sib_copy(buf, ss, rs, p, into):
        return remote(
            buf.at[pair_rows(p)], buf.at[sib_rows(into)], ss.at[into], rs.at[into], sibling
        )

    class Blocks:
        def __init__(self, buf, ss, rs, bs, br):
            self.buf, self.ss, self.rs, self.bs, self.br = buf, ss, rs, bs, br

        def copy(self, p):
            return remote(
                self.buf.at[0:T], self.buf.at[pair_rows(p)], self.ss.at[p], self.rs.at[p],
                at(chip - step(p, sgn), core),
            )

        def start_own(self):
            self.sib(0).start()
            for p in ORDER[1:]:
                self.copy(p).start()

        def sib(self, p):
            return sib_copy(self.buf, self.bs, self.br, p, 7 if p == 8 else p)

        def arrive(self, *ps):
            for p in ps:
                self.copy(p).wait_recv()
                if p != 7:
                    self.sib(p).start()

        def sib_arrived(self, p):
            if p != 8:
                self.sib(8 if p == 7 else p).wait_recv()

        def drain(self):
            for p in range(9):
                if p > 0:
                    self.copy(p).wait_send()
                if p != 7:
                    self.sib(p).wait_send()

    def span(group):
        return slice(512 * group, 512 * (group + 1))

    class Swap:
        def __init__(self, out, buf, sems):
            self.out, self.buf, self.sems = out, buf, sems
            self.rows = pl.ds(pl.multiple_of(y * T, T), T)

        def copy(self, o):
            return remote(
                self.out.at[lax.rem(y + o, 4)], self.buf.at[self.rows],
                self.sems.at[0, o], self.sems.at[1, o], column(o),
            )

        def start(self):
            for o in (2, 1, 3):
                self.copy(o).start()
            self.buf[self.rows, :] = self.out[y]

        def arrived(self):
            for o in (2, 1, 3):
                self.copy(o).wait_recv()

        def drain(self):
            for o in (1, 2, 3):
                self.copy(o).wait_send()

    class Planes:
        def __init__(self, buf, sems):
            self.buf, self.sems = buf, sems

        def move(self, into):
            src, dev = into - 1, sibling
            if into in (2, 4):
                src, dev = 0, z_peer(1 if into == 2 else 7)
            return remote(
                self.buf.at[span(src)], self.buf.at[span(into)],
                self.sems.at[0, into], self.sems.at[1, into], dev,
            )

        def start(self):
            for g in (2, 4, 1):
                self.move(g).start()

        def arrive(self, group):
            self.move(group).wait_recv()
            if group in (2, 4):
                self.move(group + 1).start()

        def drain(self):
            for g in range(1, 6):
                self.move(g).wait_send()

    swaps = [Swap(kvo, kvm, kvosems), Swap(qo, qsw, qosems), Swap(go, agm, gosems)]
    plane_keys = Planes(kvm, kvmsems)
    plane_queries = Planes(qgm, qgmsems)
    keys = Blocks(kv, kvsend, kvrecv, kvbsend, kvbrecv)
    queries = Blocks(qg, qgsend, qgrecv, qgbsend, qgbrecv)
    swaps[0].start()

    def spread(out, last, parts):
        for h in range(5):
            tile = jnp.transpose(jnp.concatenate(parts(slice(D * h, D * (h + 1))), axis=0))
            if h < 4:
                out[h] = tile
            else:
                last[...] = tile

    nothing = jnp.zeros((D, T), BF16)
    query = project(0)
    spread(qo, q4, lambda part: [query[part], nothing])
    swaps[1].start()
    swaps[0].arrived()
    plane_keys.start()
    keys.start_own()

    for o in (1, 2, 3):
        adj_copy(o).wait_recv()
    rows4 = jnp.concatenate([adjq[i, 0:1, :] for i in range(4)], axis=0)
    lane4 = lax.broadcasted_iota(jnp.int32, (4, T), 1)
    sub4 = lax.broadcasted_iota(jnp.int32, (4, T), 0)

    def view_of(group, i):
        plane = lax.rem(z + (0, 7, 1)[group // 2], 8)
        return plane * 8 + 2 * i + (core if group % 2 == 0 else 1 - core)

    for g in range(6):
        for i in range(4):
            one = jnp.sum(jnp.where(lane4 == view_of(g, i), rows4, 0.0), axis=1, keepdims=True)
            wq[2 * g + i // 2, 0:4, T * (i % 2) : T * (i % 2 + 1)] = jnp.broadcast_to(one, (4, T))

    eighth = jnp.asarray(0.125, BF16)
    swaps[1].arrived()
    a4q[...] = q4[...] * eighth
    tile = kv[0:T, :]
    a4kv[0:T, :] = jnp.where(left, tile * eighth, jnp.zeros_like(tile))
    a4kv[T : 2 * T, :] = jnp.where(left, jnp.zeros_like(tile), tile)
    quarters = [slice(T * i, T * (i + 1)) for i in range(4)]
    for part in quarters:
        aqm[part, :] = qsw[part, :] * eighth
        tile = kvm[part, :]
        akm[part, :] = jnp.where(left, tile * eighth, jnp.zeros_like(tile))
        avm[part, :] = jnp.where(left, jnp.zeros_like(tile), tile)

    loads[5].wait()
    loads[4].wait()
    for o in (1, 2, 3):
        og_copy(o).wait_recv()
    grad_att = mm(wo[...], ogt[...]).astype(BF16)
    spread(go, a4g, lambda part: [nothing, grad_att[part]])
    swaps[2].start()
    qg[0:T, :] = jnp.where(left, q4[...], a4g[...])

    for ref in (om, dqm, dkm, dvm, o4acc, dq4, dkv4):
        ref[...] = jnp.zeros_like(ref)

    def block(buf, p, n):
        return buf[pl.ds(pl.multiple_of(p * 256, 256), n), :]

    def forward(p, n):
        kv4 = block(kv, p, n)
        weight = wtab[pl.ds(p, 1), 0:n]
        ones = jnp.ones((n, T), BF16)
        e = jnp.where(weight > 0.0, jnp.exp(mm_nt(a4q[...], kv4)), 0.0).astype(BF16)
        est4[p, :, 0:n] = e
        o4acc[...] += mm(e, jnp.concatenate([kv4, ones], axis=1))

    def masked(weights, e):
        parts = [
            jnp.where(weights[i : i + 1, :] > 0.0, e[T * i : T * (i + 1)], 0.0) for i in range(4)
        ]
        return jnp.concatenate(parts, axis=0)

    def forward_plane(t):
        tile = block(kvm, t, 256)
        e = masked(wq[t], jnp.exp(mm_nt(aqm[...], tile))).astype(BF16)
        estm[t] = e
        om[...] += mm(e, jnp.concatenate([tile, jnp.ones((256, T), BF16)], axis=1))

    def run(work, blocks, order):
        for p in order:
            if blocks is not None:
                blocks.sib_arrived(p)
            work(p, T if p == 8 else 256)

    def run_plane(work, *groups):
        for g in groups:
            pl.loop(2 * g, 2 * g + 2)(work)

    run_plane(forward_plane, 0)
    swaps[2].arrived()
    for part in quarters:
        qgm[part, :] = jnp.where(left, qsw[part, :], agm[part, :])
    plane_queries.start()
    queries.start_own()
    plane_keys.arrive(2)
    plane_keys.arrive(4)
    plane_keys.arrive(1)
    run_plane(forward_plane, 1, 2, 4)
    for p in ORDER[1:]:
        keys.arrive(p)
    plane_keys.arrive(3)
    plane_keys.arrive(5)
    run_plane(forward_plane, 3, 5)
    run(forward, keys, ORDER)

    def put(stats, i, column):
        return jnp.where(lane == i, column, stats)

    stats = jnp.zeros((T, T), F32)
    invm[...] = 1.0 / om[:, T : 2 * T]
    attm = []
    for i in range(4):
        part = slice(T * i, T * (i + 1))
        own = (om[part, 0:T] * invm[part, :]).astype(BF16)
        attm.append(own)
        prod = own.astype(F32) * qgm[part, :].astype(F32)
        delta = jnp.sum(jnp.where(left, 0.0, prod), axis=1, keepdims=True)
        delm[part, :] = jnp.broadcast_to(delta, (T, T))
        stats = put(stats, i, invm[part, :])
        stats = put(stats, 4 + i, delta)
    inv = 1.0 / o4acc[:, T : 2 * T]
    inv4[...] = inv
    last = (o4acc[:, 0:T] * inv).astype(BF16)
    att[:, 256:320] = last[:, D:T]
    prod = last.astype(F32) * qg[0:T, :].astype(F32)
    delta = jnp.sum(jnp.where(left, 0.0, prod), axis=1, keepdims=True)
    del4[...] = jnp.broadcast_to(delta, (T, T))
    stats = put(stats, 16, inv)
    stats = put(stats, 17, delta)
    stats = jnp.transpose(stats)
    stm[0, 0:8, :] = stats[0:8, :]
    stm[0, 8:16, :] = jnp.concatenate([rows4, rows4], axis=0)
    st[0, 0] = stats[16:32, :]
    st[0, 0, 10:11, :] = row

    def stm_copy(i):
        dev, src, into = (
            (sibling, 0, slice(1, 2)), (z_peer(1), 0, slice(2, 4)), (z_peer(7), 0, slice(4, 6))
        )[i]
        src = slice(0, into.stop - into.start)
        return remote(stm.at[src], stm.at[into], stmsems.at[0, i], stmsems.at[1, i], dev)

    def stb_copy():
        return remote(st.at[0, 0], st.at[0, 1], stsend.at[0], strecv.at[0], sibling)

    def st_copy(p):
        return remote(
            st.at[0], st.at[p], stsend.at[p], strecv.at[p], at(chip - step(p, sgn), core)
        )

    stm_copy(0).start()
    stb_copy().start()

    def wide(a, n):
        return a if n == T else jnp.concatenate([a, a], axis=1)

    def backward_q(p, n):
        kv4 = block(kv, p, n)
        prob = est4[p, :, 0:n].astype(F32) * wide(inv4[...], n)
        dl = prob * (mm_nt(a4g[...], kv4) - wide(del4[...], n))
        dq4[...] += mm(dl.astype(BF16), kv4)

    def backward_q_plane(t):
        tile = block(kvm, t, 256)
        prob = estm[t].astype(F32) * wide(invm[...], 256)
        dl = prob * (mm_nt(agm[...], tile) - wide(delm[...], 256))
        dqm[...] += mm(dl.astype(BF16), tile)

    run_plane(backward_q_plane, 0)
    stm_copy(0).wait_recv()
    for i in (1, 2):
        stm_copy(i).start()
    run_plane(backward_q_plane, 1)
    stb_copy().wait_recv()
    for p in ORDER[1:]:
        st_copy(p).start()
    run_plane(backward_q_plane, 2, 3, 4, 5)

    def ret_copy(k, o):
        return remote(
            ret.at[k, lax.rem(y + o, 4)], retbuf.at[k, y],
            retsems.at[0, k, o], retsems.at[1, k, o], column(o),
        )

    def give_back(k, parts):
        for i in range(4):
            ret[k, i] = parts[i]
        for o in (2, 1, 3):
            ret_copy(k, o).start()
        retbuf[k, y] = ret[k, y]

    def given_back(k):
        for o in (1, 2, 3):
            ret_copy(k, o).wait_recv()

    give_back(
        0,
        [
            jnp.where(left, dqm[T * i : T * (i + 1), :] * 0.125, attm[i].astype(F32)).astype(BF16)
            for i in range(4)
        ],
    )
    run(backward_q, None, ORDER)
    gs[0, :, 256:320] = (dq4[:, 0:D] * 0.125).astype(BF16)
    plane_queries.arrive(2)
    plane_queries.arrive(4)
    plane_queries.arrive(1)
    for p in ORDER[1:]:
        queries.arrive(p)
    class Adapters:
        def __init__(
            self, which, lgsrc, lgbuf, acc, accb, other, half, halfb, rsbuf, zbuf, fin, sems
        ):
            self.which, self.lgsrc, self.lgbuf, self.acc, self.accb = which, lgsrc, lgbuf, acc, accb
            self.other, self.half, self.halfb = other, half, halfb
            self.rsbuf, self.zbuf, self.fin, self.sems = rsbuf, zbuf, fin, sems
            self.count = R * len(which)
            self.share = self.count // 4
            self.spot = core * 4 + y

        def part(self, i):
            return pl.ds(pl.multiple_of(i * self.share, 16), self.share)

        def core_rows(self, k):
            return pl.ds(pl.multiple_of(k * self.count, 64), self.count)

        def copies(self, stage):
            def copy(o):
                ends = {
                    0: lambda: (self.lgsrc, self.lgbuf.at[o], x_peer(o)),
                    1: lambda: (self.accb.at[self.core_rows(1 - core)], self.other, sibling),
                    2: lambda: (
                        self.halfb.at[self.part(lax.rem(y + o, 4))], self.rsbuf.at[o], column(o)
                    ),
                    3: lambda: (self.zbuf.at[z], self.zbuf.at[z], z_peer(o)),
                    4: lambda: (self.fin.at[self.spot], self.fin.at[self.spot], column(o)),
                    5: lambda: (
                        self.fin.at[pl.ds(4 * core, 4)], self.fin.at[pl.ds(4 * core, 4)], sibling
                    ),
                }
                src, dst, dev = ends[stage]()
                return remote(src, dst, self.sems.at[stage, 0, o], self.sems.at[stage, 1, o], dev)

            far = {1: (1,), 3: (4, 3, 5, 2, 6, 1, 7), 5: (1,)}
            return [copy(o) for o in far.get(stage, (2, 1, 3))]

        def start(self, stage):
            for c in self.copies(stage):
                c.start()

        def wait(self, stage):
            for c in self.copies(stage):
                c.wait_recv()

        def send_low(self):
            for i, m in enumerate(self.which):
                one = 0.5 * mm_nt(up[R * m : R * (m + 1), :], gs[m])
                self.lgsrc[R * i : R * (i + 1), :] = one.astype(BF16)
            self.start(0)
            for i, m in enumerate(self.which):
                self.acc[self.count + R * i : self.count + R * (i + 1), :] = 0.5 * mm(
                    low[R * m : R * (m + 1), :], gs[m]
                )

        def send_plane(self):
            self.wait(0)
            lg = self.lgsrc[...].astype(F32)
            for o in (1, 2, 3):
                lg = lg + self.lgbuf[o].astype(F32)
            lg = lg.astype(BF16)
            lgall[R * self.which[0] : R * self.which[0] + self.count, :] = lg
            self.acc[0 : self.count, :] = mm_nt(lg, xt[mine, :])
            self.accb[...] = self.acc[...].astype(BF16)
            self.start(1)

        def send_column(self):
            self.wait(1)
            self.half[...] = self.acc[self.core_rows(core), :] + self.other[...].astype(F32)
            self.halfb[...] = self.half[...].astype(BF16)
            self.start(2)

        def send_z(self):
            self.wait(2)
            total = self.half[self.part(y), :]
            for o in range(1, 4):
                total = total + self.rsbuf[o].astype(F32)
            self.zbuf[z] = total.astype(BF16)
            self.start(3)

        def send_back(self):
            self.wait(3)
            total = self.zbuf[0].astype(F32)
            for i in range(1, 8):
                total = total + self.zbuf[i].astype(F32)
            self.fin[self.spot] = total.astype(BF16)
            self.start(4)

        def finish(self):
            self.wait(4)
            self.start(5)
            self.wait(5)
            for i in range(8):
                for r in range(0, self.share, 16):
                    which, at_row = divmod((i % 4) * self.share + r, R)
                    out = ga_ref if i < 4 else gb_ref
                    rows = slice(at_row, at_row + 16)
                    out[self.which[which], rows, :] = self.fin[i, r : r + 16, :].astype(F32)

        def drain(self, *stages):
            for stage in stages:
                for c in self.copies(stage):
                    c.wait_send()

    early = Adapters((0,), *parts[:11])
    late = Adapters((1, 2), *parts[11:])

    me_lane = lax.broadcasted_iota(jnp.int32, (1, T), 1) == view

    def backward_kv(p, n):
        qg4 = block(qg, p, n)
        sides = [st[p, s] for s in range(n // T)]
        w = [jnp.sum(jnp.where(me_lane, s[10:11, :], 0.0), axis=1, keepdims=True) for s in sides]
        w = [jnp.broadcast_to(one, (1, T)) for one in w]
        w = w[0] if n == T else jnp.concatenate(w, axis=1)
        sides = sides[0] if n == T else jnp.concatenate(sides, axis=1)
        both = mm_nt(a4kv[...], qg4)
        prob = jnp.where(w > 0.0, jnp.exp(both[0:T]) * sides[0:1, :], 0.0)
        dl = prob * (both[T : 2 * T] - sides[1:2, :])
        dkv4[...] += mm(jnp.concatenate([dl, prob], axis=0).astype(BF16), qg4)

    mine4 = z * 8 + 2 * sub4 + core

    def mask_kv(g):
        for i in range(4):
            line = jnp.broadcast_to(stm[g, 8 + i : 9 + i, :], (4, T))
            one = jnp.sum(jnp.where(lane4 == mine4, line, 0.0), axis=1, keepdims=True)
            wk[2 * g + i // 2, 0:4, T * (i % 2) : T * (i % 2 + 1)] = jnp.broadcast_to(one, (4, T))

    def backward_kv_plane(g):
        mask_kv(g)
        for half in range(2):
            t = 2 * g + half
            tile = block(qgm, t, 256)
            i = 2 * half
            inv = jnp.concatenate([stm[g, i : i + 1, :], stm[g, i + 1 : i + 2, :]], axis=1)
            delta = jnp.concatenate([stm[g, 4 + i : 5 + i, :], stm[g, 5 + i : 6 + i, :]], axis=1)
            prob = masked(wk[t], jnp.exp(mm_nt(akm[...], tile)) * inv)
            dl = prob * (mm_nt(avm[...], tile) - delta)
            dkm[...] += mm(dl.astype(BF16), tile)
            dvm[...] += mm(prob.astype(BF16), tile)

    def run_kv(*order):
        for p in order:
            if p != 0:
                st_copy(p).wait_recv()
        run(backward_kv, queries, order)

    backward_kv_plane(0)
    backward_kv_plane(1)
    for i in (1, 2):
        stm_copy(i).wait_recv()
    backward_kv_plane(2)
    backward_kv_plane(4)
    plane_queries.arrive(3)
    plane_queries.arrive(5)
    backward_kv_plane(3)
    backward_kv_plane(5)
    give_back(
        1,
        [
            jnp.where(left, dkm[T * i : T * (i + 1), :] * 0.125, dvm[T * i : T * (i + 1), :]).astype(
                BF16
            )
            for i in range(4)
        ],
    )
    run_kv(*ORDER)
    given_back(0)
    for h in range(4):
        gs[0, :, D * h : D * (h + 1)] = retbuf[0, h, :, 0:D]
        att[:, D * h : D * (h + 1)] = retbuf[0, h, :, D:T]

    early.send_low()
    inacc[...] = mm(gs[0], wqkv[0:W, :])
    gs[1, :, 256:320] = (dkv4[0:T, 0:D] * 0.125).astype(BF16)
    gs[2, :, 256:320] = dkv4[T : 2 * T, D:T].astype(BF16)
    given_back(1)
    for h in range(4):
        gs[1, :, D * h : D * (h + 1)] = retbuf[1, h, :, 0:D]
        gs[2, :, D * h : D * (h + 1)] = retbuf[1, h, :, D:T]

    late.send_low()
    early.send_plane()

    share = inacc[...] + mm(gs[1], wqkv[W : 2 * W, :]) + mm(gs[2], wqkv[2 * W : 3 * W, :])
    share = share.astype(BF16)
    for h in range(4):
        gisrc[h] = share[:, W * h : W * (h + 1)]

    def gi_copy(o):
        return remote(
            gisrc.at[lax.rem(head + o, 4)], gibuf.at[o], gisend.at[o], girecv.at[o], x_peer(o)
        )

    for o in (1, 2, 3):
        gi_copy(o).start()

    share = mm(att[...], wo[...]).astype(BF16)
    for h in range(4):
        losrc[h] = share[:, W * h : W * (h + 1)]

    def lo_copy(o):
        return remote(
            losrc.at[lax.rem(head + o, 4)], lobuf.at[o], losend.at[o], lorecv.at[o], x_peer(o)
        )

    for o in (1, 2, 3):
        lo_copy(o).start()
    early.send_column()
    late.send_plane()
    early.send_z()
    late.send_column()
    late.send_z()

    own = gisrc[head].astype(F32)
    for o in (1, 2, 3):
        gi_copy(o).wait_recv()
        own = own + gibuf[o].astype(F32)
    gi_ref[0] = (jnp.transpose(own) + mm(downn[mine, :], lgall[...])).astype(BF16)
    out = losrc[head].astype(F32)
    for o in (1, 2, 3):
        lo_copy(o).wait_recv()
        out = out + lobuf[o].astype(F32)
    lo_ref[0] = jnp.transpose(out).astype(BF16)

    for o in (1, 2, 3):
        x_copy(o).wait_send()
        og_copy(o).wait_send()
        lo_copy(o).wait_send()
        gi_copy(o).wait_send()
    keys.drain()
    queries.drain()
    plane_keys.drain()
    plane_queries.drain()
    for swap in swaps:
        swap.drain()
    for o in (1, 2, 3):
        adj_copy(o).wait_send()
        ret_copy(0, o).wait_send()
        ret_copy(1, o).wait_send()
    for i in range(3):
        stm_copy(i).wait_send()

    stb_copy().wait_send()
    for p in ORDER[1:]:
        st_copy(p).wait_send()
    for part in (early, late):
        part.drain(0, 1, 2)

    early.send_back()
    late.send_back()
    early.finish()
    late.finish()

    for part in (early, late):
        part.drain(3, 4, 5)


def hand_over(*refs):
    source, target, held, sem = refs[0:4], refs[4:8], refs[8:12], refs[12]
    into = [pltpu.make_async_copy(s, h, sem.at[0, i]) for i, (s, h) in enumerate(zip(source, held))]
    out = [pltpu.make_async_copy(h, t, sem.at[1, i]) for i, (h, t) in enumerate(zip(held, target))]
    for copy in into:
        copy.start()
    for first, second in zip(into, out):
        first.wait()
        second.start()
    for copy in out:
        copy.wait()


def body(inputs, output_gradient, wqkv, wo, down, up, adjacent):
    vmem = pltpu.VMEM
    dma = pltpu.SemaphoreType.DMA
    scratch = [
        vmem((3 * W, 1280), BF16), vmem((W, 1280), BF16), vmem((3 * R, 1280), BF16),
        vmem((3 * R, W), BF16), dma((6,)),
        vmem((1280, T), BF16), vmem((1280, T), BF16), vmem((3, W, R), BF16),
        vmem((1280, 3 * R), BF16), dma((4,)), dma((4,)), dma((4,)), dma((4,)),
        vmem((4, T, T), BF16), vmem((4, T, T), BF16), vmem((4, T, T), BF16), vmem((512, T), BF16),
        vmem((T, T), BF16), dma((2, 4)), dma((2, 4)), dma((2, 4)), vmem((24 * T, T), BF16),
        vmem((24 * T, T), BF16), dma((2, 6)), dma((2, 6)), vmem((4, 8, T), F32), dma((2, 4)),
        vmem((6, 16, T), F32), dma((2, 3)), vmem((2, 4, T, T), BF16), vmem((2, 4, T, T), BF16),
        dma((2, 2, 4)),
        vmem((512, T), BF16), vmem((512, T), BF16), vmem((512, T), BF16), vmem((512, T), BF16),
        vmem((12, 8, 256), F32), vmem((12, 8, 256), F32), vmem((12, 512, 256), BF16),
        vmem((512, 256), F32), vmem((512, T), F32), vmem((512, T), F32), vmem((512, T), F32),
        vmem((512, T), F32), vmem((512, T), F32),
        vmem((17 * T, T), BF16), vmem((17 * T, T), BF16),
        dma((9,)), dma((9,)), dma((8,)), dma((8,)), dma((9,)), dma((9,)), dma((8,)), dma((8,)),
        vmem((9, 2, 16, T), F32), dma((9,)), dma((9,)),
        vmem((T, T), BF16), vmem((T, T), BF16), vmem((256, T), BF16), vmem((16, 256), F32),
        vmem((9, T, 256), BF16), vmem((T, 256), F32), vmem((T, T), F32), vmem((T, T), F32),
        vmem((T, T), F32), vmem((256, T), F32),
        vmem((T, W), BF16), vmem((3, T, W), BF16), vmem((3 * R, T), BF16), vmem((T, 1280), F32),
        vmem((4, T, W), BF16), vmem((4, T, W), BF16), dma((4,)), dma((4,)),
        vmem((4, T, W), BF16), vmem((4, T, W), BF16), dma((4,)), dma((4,)), vmem((3 * R, T), BF16),
    ]
    for count in (R, 2 * R):
        share, half = vmem((8, count // 4, W), BF16), vmem((count, W), BF16)
        scratch += [vmem((count, T), BF16), vmem((4, count, T), BF16), vmem((2 * count, W), F32)]
        scratch += [vmem((2 * count, W), BF16), half, vmem((count, W), F32), half]
        scratch += [share, share, share, dma((6, 2, 8))]
    whole = pl.BlockSpec(memory_space=pltpu.VMEM)
    hbm = pl.BlockSpec(memory_space=pltpu.HBM)
    results = pl.pallas_call(
        kernel,
        out_shape=(
            jax.ShapeDtypeStruct((1, W, T), BF16),
            jax.ShapeDtypeStruct((1, W, T), BF16),
            jax.ShapeDtypeStruct((3, R, W), F32),
            jax.ShapeDtypeStruct((3, R, W), F32),
        ),
        in_specs=[whole] + [hbm] * 6,
        out_specs=(whole,) * 4,
        scratch_shapes=scratch,
        compiler_params=pltpu.CompilerParams(
            collective_id=0, has_side_effects=True, vmem_limit_bytes=62 * 1024 * 1024
        ),
        name="layer",
    )(
        adjacent,
        jnp.swapaxes(inputs, 1, 2),
        jnp.swapaxes(output_gradient, 1, 2),
        jnp.swapaxes(wqkv, 1, 2).reshape(3 * W, 1280),
        wo,
        jnp.swapaxes(down, 1, 2).reshape(3 * R, 1280),
        up.reshape(3 * R, W),
    )
    layer_out, grad_inputs, grad_a, grad_b = pl.pallas_call(
        hand_over,
        out_shape=tuple(jax.ShapeDtypeStruct(r.shape, r.dtype) for r in results),
        in_specs=[hbm] * 4,
        out_specs=(hbm,) * 4,
        scratch_shapes=[vmem(r.shape, r.dtype) for r in results] + [dma((2, 4))],
        compiler_params=pltpu.CompilerParams(vmem_limit_bytes=62 * 1024 * 1024),
        name="hand_over",
    )(*results)
    return (
        jnp.swapaxes(layer_out, 1, 2),
        jnp.swapaxes(grad_inputs, 1, 2),
        jnp.swapaxes(grad_a, 1, 2),
        grad_b,
    )


def solution(mesh):
    return jax.shard_map(
        body,
        mesh=mesh,
        in_specs=(
            P("view", None, "head"),
            P("view", None, "head"),
            P(None, None, "head"),
            P("head", None),
            P(),
            P(None, None, "head"),
            P("view", None),
        ),
        out_specs=(
            P("view", None, "head"),
            P("view", None, "head"),
            P(None, "head", None),
            P(None, None, "head"),
        ),
        check_vma=False,
    )
```

```python
import jax
import jax.numpy as jnp
from jax import lax
from jax.experimental import pallas as pl
from jax.experimental.pallas import tpu as pltpu
from jax.sharding import PartitionSpec as P

MESH = pl.DeviceIdType.MESH
F32 = jnp.float32
BF16 = jnp.bfloat16
T = 128
W = 320
D = 64
R = 64
ORDER = (0, 3, 4, 1, 2, 5, 6, 8, 7)
CHIPS = 32


def mm(a, b):
    return lax.dot_general(a, b, (((1,), (0,)), ((), ())), preferred_element_type=F32)


def mm_nt(a, b):
    return lax.dot_general(a, b, (((1,), (1,)), ((), ())), preferred_element_type=F32)


def kernel(
    adj_ref, x_hbm, og_hbm, wqkv_hbm, wo_hbm, down_hbm, up_hbm,
    lo_ref, gi_ref, ga_ref, gb_ref,
    wqkv, wo, down, up, wsem,
    xt, ogt, upt, downn, xsend, xrecv, ogsend, ogrecv,
    kvo, qo, go, qsw, q4, kvosems, qosems, gosems, kvm, qgm, kvmsems, qgmsems, adjq, adjsems, stm, stmsems, ret, retbuf, retsems,
    aqm, agm, akm, avm, wq, wk, estm, om, invm, delm, dqm, dkm, dvm,
    kv, qg, kvsend, kvrecv, kvbsend, kvbrecv, qgsend, qgrecv, qgbsend, qgbrecv,
    st, stsend, strecv,
    a4q, a4g, a4kv, wtab, est4, o4acc, inv4, del4, dq4, dkv4,
    att, gs, low, inacc, losrc, lobuf, losend, lorecv,
    gisrc, gibuf, gisend, girecv, lgall, *parts,
):
    view = lax.axis_index("view")
    head = lax.axis_index("head")
    chip = view // 2
    core = lax.rem(view, 2)
    z = view // 8
    y = lax.rem(chip, 4)
    spot = lax.rem(view, 8)
    sgn = 2 * core - 1

    def at(c, k):
        return (lax.rem(c + 2 * CHIPS, CHIPS) * 2 + k, head)

    def step(p, side):
        near = ((p + 1) // 2) * (2 * lax.rem(p, 2) - 1)
        if isinstance(p, int):
            return {7: 4 * side, 8: -4 * side}.get(p, near)
        return jnp.where(p == 7, 4 * side, jnp.where(p == 8, -4 * side, near))

    sibling = (chip * 2 + 1 - core, head)

    def z_peer(o):
        return (lax.rem(z + o, 8) * 8 + spot, head)

    def x_peer(o):
        return (view, lax.rem(head + o, 4))

    def remote(src, dst, ss, rs, dev):
        return pltpu.make_async_remote_copy(
            src_ref=src, dst_ref=dst, send_sem=ss, recv_sem=rs,
            device_id=dev, device_id_type=MESH,
        )

    mine = pl.ds(pl.multiple_of(head * W, 64), W)
    loads = [
        pltpu.make_async_copy(s, d, wsem.at[i])
        for i, (s, d) in enumerate(
            (
                (x_hbm.at[0], xt.at[mine]), (down_hbm, down), (up_hbm, up), (wqkv_hbm, wqkv),
                (og_hbm.at[0], ogt.at[mine]), (wo_hbm, wo),
            )
        )
    ]
    loads[0].start()

    barrier = pltpu.get_barrier_semaphore()

    def greet(dev):
        pl.semaphore_signal(barrier, inc=1, device_id=dev, device_id_type=MESH)

    for o in (1, 2, 3):
        greet(x_peer(o))

    @pl.loop(1, 9)
    def _(o):
        greet((lax.rem(view + o, 64), head))
        greet((lax.rem(view + 64 - o, 64), head))

    for o in (2, 3, 4, 5, 6):
        greet(z_peer(o))
    pl.semaphore_wait(barrier, 24)

    def x_copy(o):
        return remote(x_hbm.at[0], xt.at[mine], xsend.at[o], xrecv.at[o], x_peer(o))

    def og_copy(o):
        return remote(og_hbm.at[0], ogt.at[mine], ogsend.at[o], ogrecv.at[o], x_peer(o))

    for o in (2, 1, 3):
        x_copy(o).start()
    for load in loads[1:]:
        load.start()

    adj = adj_ref[...].astype(F32)
    lane64 = lax.broadcasted_iota(jnp.int32, (1, 64), 1)

    def weight_of(v):
        one = jnp.sum(jnp.where(lane64 == v, adj, 0.0), axis=1, keepdims=True)
        return jnp.broadcast_to(one, (1, T))

    for p in range(9):
        c = lax.rem(chip + step(p, sgn) + 2 * CHIPS, CHIPS) * 2
        wtab[p : p + 1, 0:T] = weight_of(c + core)
        wtab[p : p + 1, T : 2 * T] = weight_of(c + 1 - core)
    lane = lax.broadcasted_iota(jnp.int32, (T, T), 1)
    left = lane < D

    def column(o):
        return (z * 8 + lax.rem(y + o, 4) * 2 + core, head)

    row = jnp.concatenate([adj, jnp.zeros((1, 64), F32)], axis=1)
    adjq[y] = jnp.broadcast_to(row, (8, T))

    def adj_copy(o):
        return remote(adjq.at[y], adjq.at[y], adjsems.at[0, o], adjsems.at[1, o], column(o))

    for o in (2, 1, 3):
        adj_copy(o).start()

    for load in loads[1:3]:
        load.wait()
    for m in range(3):
        upt[m] = jnp.transpose(up[R * m : R * (m + 1), :])
    for h in range(10):
        downn[T * h : T * (h + 1), :] = jnp.transpose(down[:, T * h : T * (h + 1)])

    loads[3].wait()
    loads[0].wait()
    for o in (1, 2, 3):
        x_copy(o).wait_recv()
    for o in (2, 1, 3):
        og_copy(o).start()
    low[...] = mm(down[...], xt[...]).astype(BF16)

    def project(m):
        main = mm(wqkv[W * m : W * (m + 1), :], xt[...])
        return (main + 0.5 * mm(upt[m], low[R * m : R * (m + 1), :])).astype(BF16)

    def lay_out(out, buf, first, second):
        for h in range(5):
            part = slice(D * h, D * (h + 1))
            tile = jnp.transpose(jnp.concatenate([first[part], second[part]], axis=0))
            if h < 4:
                out[h] = tile
            else:
                buf[0:T, :] = tile

    lay_out(kvo, kv, project(1), project(2))

    def pair_rows(p):
        return pl.ds(pl.multiple_of(p * 256, 256), T)

    def sib_rows(p):
        return pl.ds(pl.multiple_of(p * 256 + T, T), T)

    def sib_copy(buf, ss, rs, p, into):
        return remote(
            buf.at[pair_rows(p)], buf.at[sib_rows(into)], ss.at[into], rs.at[into], sibling
        )

    class Blocks:
        def __init__(self, buf, ss, rs, bs, br):
            self.buf, self.ss, self.rs, self.bs, self.br = buf, ss, rs, bs, br

        def copy(self, p):
            return remote(
                self.buf.at[0:T], self.buf.at[pair_rows(p)], self.ss.at[p], self.rs.at[p],
                at(chip - step(p, sgn), core),
            )

        def start_own(self):
            self.sib(0).start()
            for p in ORDER[1:]:
                self.copy(p).start()

        def sib(self, p):
            return sib_copy(self.buf, self.bs, self.br, p, 7 if p == 8 else p)

        def arrive(self, *ps):
            for p in ps:
                self.copy(p).wait_recv()
                if p != 7:
                    self.sib(p).start()

        def sib_arrived(self, p):
            if p != 8:
                self.sib(8 if p == 7 else p).wait_recv()

        def drain(self):
            for p in range(9):
                if p > 0:
                    self.copy(p).wait_send()
                if p != 7:
                    self.sib(p).wait_send()

    def span(group):
        return slice(512 * group, 512 * (group + 1))

    class Swap:
        def __init__(self, out, buf, sems):
            self.out, self.buf, self.sems = out, buf, sems
            self.rows = pl.ds(pl.multiple_of(y * T, T), T)

        def copy(self, o):
            return remote(
                self.out.at[lax.rem(y + o, 4)], self.buf.at[self.rows],
                self.sems.at[0, o], self.sems.at[1, o], column(o),
            )

        def start(self):
            for o in (2, 1, 3):
                self.copy(o).start()
            self.buf[self.rows, :] = self.out[y]

        def arrived(self):
            for o in (2, 1, 3):
                self.copy(o).wait_recv()

        def drain(self):
            for o in (1, 2, 3):
                self.copy(o).wait_send()

    class Planes:
        def __init__(self, buf, sems):
            self.buf, self.sems = buf, sems

        def move(self, into):
            src, dev = into - 1, sibling
            if into in (2, 4):
                src, dev = 0, z_peer(1 if into == 2 else 7)
            return remote(
                self.buf.at[span(src)], self.buf.at[span(into)],
                self.sems.at[0, into], self.sems.at[1, into], dev,
            )

        def start(self):
            for g in (2, 4, 1):
                self.move(g).start()

        def arrive(self, group):
            self.move(group).wait_recv()
            if group in (2, 4):
                self.move(group + 1).start()

        def drain(self):
            for g in range(1, 6):
                self.move(g).wait_send()

    swaps = [Swap(kvo, kvm, kvosems), Swap(qo, qsw, qosems), Swap(go, agm, gosems)]
    plane_keys = Planes(kvm, kvmsems)
    plane_queries = Planes(qgm, qgmsems)
    keys = Blocks(kv, kvsend, kvrecv, kvbsend, kvbrecv)
    queries = Blocks(qg, qgsend, qgrecv, qgbsend, qgbrecv)
    swaps[0].start()

    def spread(out, last, parts):
        for h in range(5):
            tile = jnp.transpose(jnp.concatenate(parts(slice(D * h, D * (h + 1))), axis=0))
            if h < 4:
                out[h] = tile
            else:
                last[...] = tile

    nothing = jnp.zeros((D, T), BF16)
    query = project(0)
    spread(qo, q4, lambda part: [query[part], nothing])
    swaps[1].start()
    swaps[0].arrived()
    plane_keys.start()
    keys.start_own()

    for o in (1, 2, 3):
        adj_copy(o).wait_recv()
    rows4 = jnp.concatenate([adjq[i, 0:1, :] for i in range(4)], axis=0)
    lane4 = lax.broadcasted_iota(jnp.int32, (4, T), 1)
    sub4 = lax.broadcasted_iota(jnp.int32, (4, T), 0)

    def view_of(group, i):
        plane = lax.rem(z + (0, 7, 1)[group // 2], 8)
        return plane * 8 + 2 * i + (core if group % 2 == 0 else 1 - core)

    for g in range(6):
        for i in range(4):
            one = jnp.sum(jnp.where(lane4 == view_of(g, i), rows4, 0.0), axis=1, keepdims=True)
            wq[2 * g + i // 2, 0:4, T * (i % 2) : T * (i % 2 + 1)] = jnp.broadcast_to(one, (4, T))

    eighth = jnp.asarray(0.125, BF16)
    swaps[1].arrived()
    a4q[...] = q4[...] * eighth
    tile = kv[0:T, :]
    a4kv[0:T, :] = jnp.where(left, tile * eighth, jnp.zeros_like(tile))
    a4kv[T : 2 * T, :] = jnp.where(left, jnp.zeros_like(tile), tile)
    quarters = [slice(T * i, T * (i + 1)) for i in range(4)]
    for part in quarters:
        aqm[part, :] = qsw[part, :] * eighth
        tile = kvm[part, :]
        akm[part, :] = jnp.where(left, tile * eighth, jnp.zeros_like(tile))
        avm[part, :] = jnp.where(left, jnp.zeros_like(tile), tile)

    loads[5].wait()
    loads[4].wait()
    for o in (1, 2, 3):
        og_copy(o).wait_recv()
    grad_att = mm(wo[...], ogt[...]).astype(BF16)
    spread(go, a4g, lambda part: [nothing, grad_att[part]])
    swaps[2].start()
    qg[0:T, :] = jnp.where(left, q4[...], a4g[...])

    for ref in (om, dqm, dkm, dvm, o4acc, dq4, dkv4):
        ref[...] = jnp.zeros_like(ref)

    def block(buf, p, n):
        return buf[pl.ds(pl.multiple_of(p * 256, 256), n), :]

    def forward(p, n):
        kv4 = block(kv, p, n)
        weight = wtab[pl.ds(p, 1), 0:n]
        ones = jnp.ones((n, T), BF16)
        e = jnp.where(weight > 0.0, jnp.exp(mm_nt(a4q[...], kv4)), 0.0).astype(BF16)
        est4[p, :, 0:n] = e
        o4acc[...] += mm(e, jnp.concatenate([kv4, ones], axis=1))

    def masked(weights, e):
        parts = [
            jnp.where(weights[i : i + 1, :] > 0.0, e[T * i : T * (i + 1)], 0.0) for i in range(4)
        ]
        return jnp.concatenate(parts, axis=0)

    def forward_plane(t):
        tile = block(kvm, t, 256)
        e = masked(wq[t], jnp.exp(mm_nt(aqm[...], tile))).astype(BF16)
        estm[t] = e
        om[...] += mm(e, jnp.concatenate([tile, jnp.ones((256, T), BF16)], axis=1))

    def run(work, blocks, order):
        for p in order:
            if blocks is not None:
                blocks.sib_arrived(p)
            work(p, T if p == 8 else 256)

    def run_plane(work, *groups):
        for g in groups:
            pl.loop(2 * g, 2 * g + 2)(work)

    run_plane(forward_plane, 0)
    swaps[2].arrived()
    for part in quarters:
        qgm[part, :] = jnp.where(left, qsw[part, :], agm[part, :])
    plane_queries.start()
    queries.start_own()
    plane_keys.arrive(2)
    plane_keys.arrive(4)
    plane_keys.arrive(1)
    run_plane(forward_plane, 1, 2, 4)
    for p in ORDER[1:]:
        keys.arrive(p)
    plane_keys.arrive(3)
    plane_keys.arrive(5)
    run_plane(forward_plane, 3, 5)
    run(forward, keys, ORDER)

    def put(stats, i, column):
        return jnp.where(lane == i, column, stats)

    stats = jnp.zeros((T, T), F32)
    invm[...] = 1.0 / om[:, T : 2 * T]
    attm = []
    for i in range(4):
        part = slice(T * i, T * (i + 1))
        own = (om[part, 0:T] * invm[part, :]).astype(BF16)
        attm.append(own)
        prod = own.astype(F32) * qgm[part, :].astype(F32)
        delta = jnp.sum(jnp.where(left, 0.0, prod), axis=1, keepdims=True)
        delm[part, :] = jnp.broadcast_to(delta, (T, T))
        stats = put(stats, i, invm[part, :])
        stats = put(stats, 4 + i, delta)
    inv = 1.0 / o4acc[:, T : 2 * T]
    inv4[...] = inv
    last = (o4acc[:, 0:T] * inv).astype(BF16)
    att[:, 256:320] = last[:, D:T]
    prod = last.astype(F32) * qg[0:T, :].astype(F32)
    delta = jnp.sum(jnp.where(left, 0.0, prod), axis=1, keepdims=True)
    del4[...] = jnp.broadcast_to(delta, (T, T))
    stats = put(stats, 16, inv)
    stats = put(stats, 17, delta)
    stats = jnp.transpose(stats)
    stm[0, 0:8, :] = stats[0:8, :]
    stm[0, 8:16, :] = jnp.concatenate([rows4, rows4], axis=0)
    st[0, 0] = stats[16:32, :]
    st[0, 0, 10:11, :] = row

    def stm_copy(i):
        dev, src, into = (
            (sibling, 0, slice(1, 2)), (z_peer(1), 0, slice(2, 4)), (z_peer(7), 0, slice(4, 6))
        )[i]
        src = slice(0, into.stop - into.start)
        return remote(stm.at[src], stm.at[into], stmsems.at[0, i], stmsems.at[1, i], dev)

    def stb_copy():
        return remote(st.at[0, 0], st.at[0, 1], stsend.at[0], strecv.at[0], sibling)

    def st_copy(p):
        return remote(
            st.at[0], st.at[p], stsend.at[p], strecv.at[p], at(chip - step(p, sgn), core)
        )

    stm_copy(0).start()
    stb_copy().start()

    def wide(a, n):
        return a if n == T else jnp.concatenate([a, a], axis=1)

    def backward_q(p, n):
        kv4 = block(kv, p, n)
        prob = est4[p, :, 0:n].astype(F32) * wide(inv4[...], n)
        dl = prob * (mm_nt(a4g[...], kv4) - wide(del4[...], n))
        dq4[...] += mm(dl.astype(BF16), kv4)

    def backward_q_plane(t):
        tile = block(kvm, t, 256)
        prob = estm[t].astype(F32) * wide(invm[...], 256)
        dl = prob * (mm_nt(agm[...], tile) - wide(delm[...], 256))
        dqm[...] += mm(dl.astype(BF16), tile)

    run_plane(backward_q_plane, 0)
    stm_copy(0).wait_recv()
    for i in (1, 2):
        stm_copy(i).start()
    run_plane(backward_q_plane, 1)
    stb_copy().wait_recv()
    for p in ORDER[1:]:
        st_copy(p).start()
    run_plane(backward_q_plane, 2, 3, 4, 5)

    def ret_copy(k, o):
        return remote(
            ret.at[k, lax.rem(y + o, 4)], retbuf.at[k, y],
            retsems.at[0, k, o], retsems.at[1, k, o], column(o),
        )

    def give_back(k, parts):
        for i in range(4):
            ret[k, i] = parts[i]
        for o in (2, 1, 3):
            ret_copy(k, o).start()
        retbuf[k, y] = ret[k, y]

    def given_back(k):
        for o in (1, 2, 3):
            ret_copy(k, o).wait_recv()

    give_back(
        0,
        [
            jnp.where(left, dqm[T * i : T * (i + 1), :] * 0.125, attm[i].astype(F32)).astype(BF16)
            for i in range(4)
        ],
    )
    run(backward_q, None, ORDER)
    gs[0, :, 256:320] = (dq4[:, 0:D] * 0.125).astype(BF16)
    plane_queries.arrive(2)
    plane_queries.arrive(4)
    plane_queries.arrive(1)
    for p in ORDER[1:]:
        queries.arrive(p)
    class Adapters:
        def __init__(
            self, which, lgsrc, lgbuf, acc, accb, other, half, halfb, rsbuf, zbuf, fin, sems
        ):
            self.which, self.lgsrc, self.lgbuf, self.acc, self.accb = which, lgsrc, lgbuf, acc, accb
            self.other, self.half, self.halfb = other, half, halfb
            self.rsbuf, self.zbuf, self.fin, self.sems = rsbuf, zbuf, fin, sems
            self.count = R * len(which)
            self.share = self.count // 4
            self.spot = core * 4 + y

        def part(self, i):
            return pl.ds(pl.multiple_of(i * self.share, 16), self.share)

        def core_rows(self, k):
            return pl.ds(pl.multiple_of(k * self.count, 64), self.count)

        def copies(self, stage):
            def copy(o):
                ends = {
                    0: lambda: (self.lgsrc, self.lgbuf.at[o], x_peer(o)),
                    1: lambda: (self.accb.at[self.core_rows(1 - core)], self.other, sibling),
                    2: lambda: (
                        self.halfb.at[self.part(lax.rem(y + o, 4))], self.rsbuf.at[o], column(o)
                    ),
                    3: lambda: (self.zbuf.at[z], self.zbuf.at[z], z_peer(o)),
                    4: lambda: (self.fin.at[self.spot], self.fin.at[self.spot], column(o)),
                    5: lambda: (
                        self.fin.at[pl.ds(4 * core, 4)], self.fin.at[pl.ds(4 * core, 4)], sibling
                    ),
                }
                src, dst, dev = ends[stage]()
                return remote(src, dst, self.sems.at[stage, 0, o], self.sems.at[stage, 1, o], dev)

            far = {1: (1,), 3: (4, 3, 5, 2, 6, 1, 7), 5: (1,)}
            return [copy(o) for o in far.get(stage, (2, 1, 3))]

        def start(self, stage):
            for c in self.copies(stage):
                c.start()

        def wait(self, stage):
            for c in self.copies(stage):
                c.wait_recv()

        def send_low(self):
            for i, m in enumerate(self.which):
                one = 0.5 * mm_nt(up[R * m : R * (m + 1), :], gs[m])
                self.lgsrc[R * i : R * (i + 1), :] = one.astype(BF16)
            self.start(0)
            for i, m in enumerate(self.which):
                self.acc[self.count + R * i : self.count + R * (i + 1), :] = 0.5 * mm(
                    low[R * m : R * (m + 1), :], gs[m]
                )

        def send_plane(self):
            self.wait(0)
            lg = self.lgsrc[...].astype(F32)
            for o in (1, 2, 3):
                lg = lg + self.lgbuf[o].astype(F32)
            lg = lg.astype(BF16)
            lgall[R * self.which[0] : R * self.which[0] + self.count, :] = lg
            self.acc[0 : self.count, :] = mm_nt(lg, xt[mine, :])
            self.accb[...] = self.acc[...].astype(BF16)
            self.start(1)

        def send_column(self):
            self.wait(1)
            self.half[...] = self.acc[self.core_rows(core), :] + self.other[...].astype(F32)
            self.halfb[...] = self.half[...].astype(BF16)
            self.start(2)

        def send_z(self):
            self.wait(2)
            total = self.half[self.part(y), :]
            for o in range(1, 4):
                total = total + self.rsbuf[o].astype(F32)
            self.zbuf[z] = total.astype(BF16)
            self.start(3)

        def send_back(self):
            self.wait(3)
            total = self.zbuf[0].astype(F32)
            for i in range(1, 8):
                total = total + self.zbuf[i].astype(F32)
            self.fin[self.spot] = total.astype(BF16)
            self.start(4)

        def finish(self):
            self.wait(4)
            self.start(5)
            self.wait(5)
            for i in range(8):
                for r in range(0, self.share, 16):
                    which, at_row = divmod((i % 4) * self.share + r, R)
                    out = ga_ref if i < 4 else gb_ref
                    rows = slice(at_row, at_row + 16)
                    out[self.which[which], rows, :] = self.fin[i, r : r + 16, :].astype(F32)

        def drain(self, *stages):
            for stage in stages:
                for c in self.copies(stage):
                    c.wait_send()

    early = Adapters((0,), *parts[:11])
    late = Adapters((1, 2), *parts[11:])

    me_lane = lax.broadcasted_iota(jnp.int32, (1, T), 1) == view

    def backward_kv(p, n):
        qg4 = block(qg, p, n)
        sides = [st[p, s] for s in range(n // T)]
        w = [jnp.sum(jnp.where(me_lane, s[10:11, :], 0.0), axis=1, keepdims=True) for s in sides]
        w = [jnp.broadcast_to(one, (1, T)) for one in w]
        w = w[0] if n == T else jnp.concatenate(w, axis=1)
        sides = sides[0] if n == T else jnp.concatenate(sides, axis=1)
        both = mm_nt(a4kv[...], qg4)
        prob = jnp.where(w > 0.0, jnp.exp(both[0:T]) * sides[0:1, :], 0.0)
        dl = prob * (both[T : 2 * T] - sides[1:2, :])
        dkv4[...] += mm(jnp.concatenate([dl, prob], axis=0).astype(BF16), qg4)

    mine4 = z * 8 + 2 * sub4 + core

    def mask_kv(g):
        for i in range(4):
            line = jnp.broadcast_to(stm[g, 8 + i : 9 + i, :], (4, T))
            one = jnp.sum(jnp.where(lane4 == mine4, line, 0.0), axis=1, keepdims=True)
            wk[2 * g + i // 2, 0:4, T * (i % 2) : T * (i % 2 + 1)] = jnp.broadcast_to(one, (4, T))

    def backward_kv_plane(g):
        mask_kv(g)
        for half in range(2):
            t = 2 * g + half
            tile = block(qgm, t, 256)
            i = 2 * half
            inv = jnp.concatenate([stm[g, i : i + 1, :], stm[g, i + 1 : i + 2, :]], axis=1)
            delta = jnp.concatenate([stm[g, 4 + i : 5 + i, :], stm[g, 5 + i : 6 + i, :]], axis=1)
            prob = masked(wk[t], jnp.exp(mm_nt(akm[...], tile)) * inv)
            dl = prob * (mm_nt(avm[...], tile) - delta)
            dkm[...] += mm(dl.astype(BF16), tile)
            dvm[...] += mm(prob.astype(BF16), tile)

    def run_kv(*order):
        for p in order:
            if p != 0:
                st_copy(p).wait_recv()
        run(backward_kv, queries, order)

    backward_kv_plane(0)
    backward_kv_plane(1)
    for i in (1, 2):
        stm_copy(i).wait_recv()
    backward_kv_plane(2)
    backward_kv_plane(4)
    plane_queries.arrive(3)
    plane_queries.arrive(5)
    backward_kv_plane(3)
    backward_kv_plane(5)
    give_back(
        1,
        [
            jnp.where(left, dkm[T * i : T * (i + 1), :] * 0.125, dvm[T * i : T * (i + 1), :]).astype(
                BF16
            )
            for i in range(4)
        ],
    )
    run_kv(*ORDER)
    given_back(0)
    for h in range(4):
        gs[0, :, D * h : D * (h + 1)] = retbuf[0, h, :, 0:D]
        att[:, D * h : D * (h + 1)] = retbuf[0, h, :, D:T]

    early.send_low()
    inacc[...] = mm(gs[0], wqkv[0:W, :])
    gs[1, :, 256:320] = (dkv4[0:T, 0:D] * 0.125).astype(BF16)
    gs[2, :, 256:320] = dkv4[T : 2 * T, D:T].astype(BF16)
    given_back(1)
    for h in range(4):
        gs[1, :, D * h : D * (h + 1)] = retbuf[1, h, :, 0:D]
        gs[2, :, D * h : D * (h + 1)] = retbuf[1, h, :, D:T]

    late.send_low()
    early.send_plane()

    share = inacc[...] + mm(gs[1], wqkv[W : 2 * W, :]) + mm(gs[2], wqkv[2 * W : 3 * W, :])
    share = share.astype(BF16)
    for h in range(4):
        gisrc[h] = share[:, W * h : W * (h + 1)]

    def gi_copy(o):
        return remote(
            gisrc.at[lax.rem(head + o, 4)], gibuf.at[o], gisend.at[o], girecv.at[o], x_peer(o)
        )

    for o in (1, 2, 3):
        gi_copy(o).start()

    share = mm(att[...], wo[...]).astype(BF16)
    for h in range(4):
        losrc[h] = share[:, W * h : W * (h + 1)]

    def lo_copy(o):
        return remote(
            losrc.at[lax.rem(head + o, 4)], lobuf.at[o], losend.at[o], lorecv.at[o], x_peer(o)
        )

    for o in (1, 2, 3):
        lo_copy(o).start()
    early.send_column()
    late.send_plane()
    early.send_z()
    late.send_column()
    late.send_z()

    own = gisrc[head].astype(F32)
    for o in (1, 2, 3):
        gi_copy(o).wait_recv()
        own = own + gibuf[o].astype(F32)
    gi_ref[0] = (jnp.transpose(own) + mm(downn[mine, :], lgall[...])).astype(BF16)
    early.send_back()
    late.send_back()

    out = losrc[head].astype(F32)
    for o in (1, 2, 3):
        lo_copy(o).wait_recv()
        out = out + lobuf[o].astype(F32)
    lo_ref[0] = jnp.transpose(out).astype(BF16)

    for o in (1, 2, 3):
        x_copy(o).wait_send()
        og_copy(o).wait_send()
        lo_copy(o).wait_send()
        gi_copy(o).wait_send()
    keys.drain()
    queries.drain()
    plane_keys.drain()
    plane_queries.drain()
    for swap in swaps:
        swap.drain()
    for o in (1, 2, 3):
        adj_copy(o).wait_send()
        ret_copy(0, o).wait_send()
        ret_copy(1, o).wait_send()
    for i in range(3):
        stm_copy(i).wait_send()

    stb_copy().wait_send()
    for p in ORDER[1:]:
        st_copy(p).wait_send()
    for part in (early, late):
        part.drain(0, 1, 2)

    early.finish()
    late.finish()

    for part in (early, late):
        part.drain(3, 4, 5)


def hand_over(*refs):
    source, target, held, sem = refs[0:4], refs[4:8], refs[8:12], refs[12]
    into = [pltpu.make_async_copy(s, h, sem.at[0, i]) for i, (s, h) in enumerate(zip(source, held))]
    out = [pltpu.make_async_copy(h, t, sem.at[1, i]) for i, (h, t) in enumerate(zip(held, target))]
    for copy in into:
        copy.start()
    for first, second in zip(into, out):
        first.wait()
        second.start()
    for copy in out:
        copy.wait()


def body(inputs, output_gradient, wqkv, wo, down, up, adjacent):
    vmem = pltpu.VMEM
    dma = pltpu.SemaphoreType.DMA
    scratch = [
        vmem((3 * W, 1280), BF16), vmem((W, 1280), BF16), vmem((3 * R, 1280), BF16),
        vmem((3 * R, W), BF16), dma((6,)),
        vmem((1280, T), BF16), vmem((1280, T), BF16), vmem((3, W, R), BF16),
        vmem((1280, 3 * R), BF16), dma((4,)), dma((4,)), dma((4,)), dma((4,)),
        vmem((4, T, T), BF16), vmem((4, T, T), BF16), vmem((4, T, T), BF16), vmem((512, T), BF16),
        vmem((T, T), BF16), dma((2, 4)), dma((2, 4)), dma((2, 4)), vmem((24 * T, T), BF16),
        vmem((24 * T, T), BF16), dma((2, 6)), dma((2, 6)), vmem((4, 8, T), F32), dma((2, 4)),
        vmem((6, 16, T), F32), dma((2, 3)), vmem((2, 4, T, T), BF16), vmem((2, 4, T, T), BF16),
        dma((2, 2, 4)),
        vmem((512, T), BF16), vmem((512, T), BF16), vmem((512, T), BF16), vmem((512, T), BF16),
        vmem((12, 8, 256), F32), vmem((12, 8, 256), F32), vmem((12, 512, 256), BF16),
        vmem((512, 256), F32), vmem((512, T), F32), vmem((512, T), F32), vmem((512, T), F32),
        vmem((512, T), F32), vmem((512, T), F32),
        vmem((17 * T, T), BF16), vmem((17 * T, T), BF16),
        dma((9,)), dma((9,)), dma((8,)), dma((8,)), dma((9,)), dma((9,)), dma((8,)), dma((8,)),
        vmem((9, 2, 16, T), F32), dma((9,)), dma((9,)),
        vmem((T, T), BF16), vmem((T, T), BF16), vmem((256, T), BF16), vmem((16, 256), F32),
        vmem((9, T, 256), BF16), vmem((T, 256), F32), vmem((T, T), F32), vmem((T, T), F32),
        vmem((T, T), F32), vmem((256, T), F32),
        vmem((T, W), BF16), vmem((3, T, W), BF16), vmem((3 * R, T), BF16), vmem((T, 1280), F32),
        vmem((4, T, W), BF16), vmem((4, T, W), BF16), dma((4,)), dma((4,)),
        vmem((4, T, W), BF16), vmem((4, T, W), BF16), dma((4,)), dma((4,)), vmem((3 * R, T), BF16),
    ]
    for count in (R, 2 * R):
        share, half = vmem((8, count // 4, W), BF16), vmem((count, W), BF16)
        scratch += [vmem((count, T), BF16), vmem((4, count, T), BF16), vmem((2 * count, W), F32)]
        scratch += [vmem((2 * count, W), BF16), half, vmem((count, W), F32), half]
        scratch += [share, share, share, dma((6, 2, 8))]
    whole = pl.BlockSpec(memory_space=pltpu.VMEM)
    hbm = pl.BlockSpec(memory_space=pltpu.HBM)
    results = pl.pallas_call(
        kernel,
        out_shape=(
            jax.ShapeDtypeStruct((1, W, T), BF16),
            jax.ShapeDtypeStruct((1, W, T), BF16),
            jax.ShapeDtypeStruct((3, R, W), F32),
            jax.ShapeDtypeStruct((3, R, W), F32),
        ),
        in_specs=[whole] + [hbm] * 6,
        out_specs=(whole,) * 4,
        scratch_shapes=scratch,
        compiler_params=pltpu.CompilerParams(
            collective_id=0, has_side_effects=True, vmem_limit_bytes=62 * 1024 * 1024
        ),
        name="layer",
    )(
        adjacent,
        jnp.swapaxes(inputs, 1, 2),
        jnp.swapaxes(output_gradient, 1, 2),
        jnp.swapaxes(wqkv, 1, 2).reshape(3 * W, 1280),
        wo,
        jnp.swapaxes(down, 1, 2).reshape(3 * R, 1280),
        up.reshape(3 * R, W),
    )
    layer_out, grad_inputs, grad_a, grad_b = pl.pallas_call(
        hand_over,
        out_shape=tuple(jax.ShapeDtypeStruct(r.shape, r.dtype) for r in results),
        in_specs=[hbm] * 4,
        out_specs=(hbm,) * 4,
        scratch_shapes=[vmem(r.shape, r.dtype) for r in results] + [dma((2, 4))],
        compiler_params=pltpu.CompilerParams(vmem_limit_bytes=62 * 1024 * 1024),
        name="hand_over",
    )(*results)
    return (
        jnp.swapaxes(layer_out, 1, 2),
        jnp.swapaxes(grad_inputs, 1, 2),
        jnp.swapaxes(grad_a, 1, 2),
        grad_b,
    )


def solution(mesh):
    return jax.shard_map(
        body,
        mesh=mesh,
        in_specs=(
            P("view", None, "head"),
            P("view", None, "head"),
            P(None, None, "head"),
            P("head", None),
            P(),
            P(None, None, "head"),
            P("view", None),
        ),
        out_specs=(
            P("view", None, "head"),
            P("view", None, "head"),
            P(None, "head", None),
            P(None, None, "head"),
        ),
        check_vma=False,
    )
```
